32 devices in a mesh: dp: 8 (over z, x), head: 4 (over y, core).
Axes of the slice: x: 2, y: 2, z: 4, core: 2. Of those that a mesh axis runs over, the one named last changes fastest.
Arguments:
- layer_input: bfloat16 [256, 250, 128], P('dp'), may hold values from -6 to 6
- cotangent: bfloat16 [256, 250, 128], P('dp'), may hold values from -6 to 6
- window_count: int32 [8], P('dp'), may hold values from 1 to 32, as said below
- sample_weight: float32 [256], P('dp'), may hold values from 0.3 to 3
- ln1_gain: float32 [2, 128], replicated, may hold values from 0.5 to 1.5
- ln1_shift: float32 [2, 128], replicated, may hold values from -2 to 2
- qkv_weight: bfloat16 [2, 128, 384], P(None, None, 'head'), may hold values from -0.5 to 0.5
- qv_bias: float32 [2, 256], P(None, 'head'), may hold values from -3 to 3
- out_weight: bfloat16 [2, 128, 128], replicated, may hold values from -3 to 3
- out_bias: float32 [2, 128], replicated, may hold values from -2 to 2
- ln2_gain: float32 [2, 128], replicated, may hold values from 0.5 to 1.5
- ln2_shift: float32 [2, 128], replicated, may hold values from -2 to 2
- up_weight: bfloat16 [2, 128, 512], replicated, may hold values from -0.5 to 0.5
- up_bias: float32 [2, 512], replicated, may hold values from -3 to 3
- down_weight: bfloat16 [2, 512, 128], replicated, may hold values from -0.25 to 0.25
- down_bias: float32 [2, 128], replicated, may hold values from -2 to 2
Outputs:
- layer_out: bfloat16 [256, 250, 128], P('dp', None, 'head')
- input_grad: float32 [256, 250, 128], P('dp', None, 'head')
- ln1_gain_grad: float32 [2, 128], replicated
- ln1_shift_grad: float32 [2, 128], replicated
- qkv_weight_grad: float32 [2, 128, 384], P(None, None, 'head')
- qv_bias_grad: float32 [2, 256], P(None, 'head')
- out_weight_grad: float32 [2, 128, 128], P(None, 'head')
- out_bias_grad: float32 [2, 128], replicated
- ln2_gain_grad: float32 [2, 128], replicated
- ln2_shift_grad: float32 [2, 128], replicated
- up_weight_grad: float32 [2, 128, 512], P(None, None, 'head')
- up_bias_grad: float32 [2, 512], P(None, 'head')
- down_weight_grad: float32 [2, 512, 128], P(None, 'head')
- down_bias_grad: float32 [2, 128], replicated
The draws below stay inside these ranges and needn't reach their ends.
Inputs may be any that keep to these rules, and one draw needn't show every extreme that they name: The first window_count slots of each dp index hold real windows, the others are padding; some dp index has all 32 slots real.
All inputs are finite; a program needn't handle non-finite values.
Results may differ from the reference program's by a relative error of at most 0.019.
Values may be sent and summed in bfloat16 or wider, within the bound.
A program may use at most 384 MiB of HBM per device.

```python
import math
import jax
import jax.numpy as jnp
from jax import lax

D = 128
HEADS = 4
FF = 512
WIN = 250
LAYERS = 2
SLOTS = 32
DP_GROUPS = 8
WINDOWS = 256


def draw_window_count(key, part):
    key = jax.random.fold_in(key, 11)
    first_key, second_key = jax.random.split(key)
    counts = jax.random.randint(first_key, (DP_GROUPS,), 1, SLOTS + 1)
    full_group = jax.random.randint(second_key, (), 0, DP_GROUPS)
    return jnp.where(jnp.arange(DP_GROUPS) == full_group, SLOTS, counts).astype(jnp.int32)


def levels(key, extent, cuts, least, high):
    level, own = 1.0, jax.random.fold_in(key, 6)
    for dim, blocks in cuts:
        steps = jnp.exp(jax.random.uniform(jax.random.fold_in(own, dim), (blocks,), jnp.float32, least / len(cuts), high / len(cuts)))
        level = level * jnp.repeat(steps, extent[dim] // blocks).reshape([-1 if axis == dim else 1 for axis in range(len(extent))])
    return level


def gaussian(rng, dims, width, most, shards=(), kind=jnp.bfloat16):
    values = width * jax.random.normal(rng, dims, jnp.float32)
    if shards:
        values = values * levels(rng, dims, shards, -0.22, 0.18)
    return jnp.clip(values, -most, most).astype(kind)


def setup_inputs(seed: int = 0) -> dict:
    keys = jax.random.split(jax.random.key(seed), 17)
    return {
        "layer_input": gaussian(keys[0], (WINDOWS, WIN, D), 1.0, 6.0, ((0, 8),)),
        "cotangent": gaussian(keys[1], (WINDOWS, WIN, D), 1.0, 6.0, ((0, 8),)),
        "window_count": draw_window_count(jax.random.fold_in(keys[16], 71), 0),
        "sample_weight": jnp.clip(jnp.exp(math.log(3.0) - 2.3025851 * jax.random.uniform(keys[3], (WINDOWS,), jnp.float32) ** levels(keys[3], (WINDOWS,), ((0, 8),), -0.2, 0.2)), 0.3, 3.0),
        "ln1_gain": jnp.clip(1.0 + 0.1 * jax.random.normal(keys[4], (LAYERS, D), jnp.float32), 0.5, 1.5),
        "ln1_shift": gaussian(keys[5], (LAYERS, D), 0.3, 2.0, (), jnp.float32),
        "qkv_weight": gaussian(keys[6], (LAYERS, D, 3 * D), D ** -0.5, 0.5, ((2, 4),)),
        "qv_bias": gaussian(keys[7], (LAYERS, 2 * D), 0.5, 3.0, ((1, 4),), jnp.float32),
        "out_weight": gaussian(keys[8], (LAYERS, D, D), (max(D // 32, 1)) ** -0.5, 3.0),
        "out_bias": gaussian(keys[9], (LAYERS, D), 0.3, 2.0, (), jnp.float32),
        "ln2_gain": jnp.clip(1.0 + 0.1 * jax.random.normal(keys[10], (LAYERS, D), jnp.float32), 0.5, 1.5),
        "ln2_shift": gaussian(keys[11], (LAYERS, D), 0.3, 2.0, (), jnp.float32),
        "up_weight": gaussian(keys[12], (LAYERS, D, FF), D ** -0.5, 0.5),
        "up_bias": gaussian(keys[13], (LAYERS, FF), 0.5, 3.0, (), jnp.float32),
        "down_weight": gaussian(keys[14], (LAYERS, FF, D), FF ** -0.5, 0.25),
        "down_bias": gaussian(keys[15], (LAYERS, D), 0.3, 2.0, (), jnp.float32),
    }


@jax.custom_vjp
def low(v):
    return lax.optimization_barrier(v.astype(jnp.bfloat16)).astype(jnp.float32)

@jax.custom_vjp
def low_back(v):
    return v

def low_keep(v):
    return (low(v), None)

def low_pass(kept, grad):
    return (grad,)

def back_keep(v):
    return (v, None)

def back_low(kept, grad):
    return (low(grad),)
low.defvjp(low_keep, low_pass)
low_back.defvjp(back_keep, back_low)
norm_eps = 1e-05
window_group = 4
highest = lax.Precision.HIGHEST

def layer_norm(values, gain, shift):
    center = values - lax.optimization_barrier(jnp.mean(values, axis=-1, keepdims=True))
    spread_inv = lax.rsqrt(lax.optimization_barrier(jnp.mean(center * center, axis=-1, keepdims=True)) + norm_eps)
    return center * spread_inv * gain + shift

def attend_group(grouped):
    head_dim = D // HEADS
    queries = grouped[:, :, :, 0]
    key_rows = grouped[:, :, :, 1]
    value_rows = grouped[:, :, :, 2]
    scores = jnp.einsum('gqhd,gkhd->ghqk', queries, key_rows, precision=highest) * (1.0 / math.sqrt(head_dim))
    scores = low_back(scores)
    causal = lax.broadcasted_iota(jnp.int32, (WIN, WIN), 0) >= lax.broadcasted_iota(jnp.int32, (WIN, WIN), 1)
    scores = jnp.where(causal, scores, -1e+30)
    row_top = lax.optimization_barrier(jnp.max(scores, axis=-1, keepdims=True))
    expo = jnp.exp(scores - row_top)
    probs = low(expo / lax.optimization_barrier(jnp.sum(expo, axis=-1, keepdims=True)))
    output = jnp.einsum('ghqk,gkhd->gqhd', probs, value_rows, precision=highest)
    return output.reshape(grouped.shape[0], WIN, D)

def block_forward(stream, gain_one, shift_one, qkv_w, qv_b, out_w, out_b, gain_two, shift_two, up_w, up_b, down_w, down_b):
    head_dim = D // HEADS
    norm_one = low(layer_norm(stream, gain_one, shift_one))
    bias_pairs = qv_b.reshape(HEADS, 2, head_dim)
    bias_full = jnp.stack([bias_pairs[:, 0], jnp.zeros_like(bias_pairs[:, 0]), bias_pairs[:, 1]], axis=1).reshape(3 * D)
    projected = low_back(low(jnp.dot(norm_one, qkv_w, precision=highest) + bias_full))
    grouped = projected.reshape(WINDOWS // window_group, window_group, WIN, HEADS, 3, head_dim)
    attended = lax.map(jax.checkpoint(attend_group), grouped)
    attended = low_back(low(attended.reshape(WINDOWS * WIN, D)))
    mixed = stream + low_back(jnp.dot(attended, out_w, precision=highest) + out_b)
    norm_two = low(layer_norm(mixed, gain_two, shift_two))
    pre = low_back(jnp.dot(norm_two, up_w, precision=highest) + up_b)
    act = low(jax.nn.gelu(pre, approximate=False))
    return mixed + low_back(jnp.dot(act, down_w, precision=highest) + down_b)

def forward_all(stream, params):
    for layer_idx in range(LAYERS):
        stream = block_forward(stream, *[param[layer_idx] for param in params])
    return stream

def reference(layer_input, cotangent, window_count, sample_weight, ln1_gain, ln1_shift, qkv_weight, qv_bias, out_weight, out_bias, ln2_gain, ln2_shift, up_weight, up_bias, down_weight, down_bias):
    params = tuple((param.astype(jnp.float32) for param in (ln1_gain, ln1_shift, qkv_weight, qv_bias, out_weight, out_bias, ln2_gain, ln2_shift, up_weight, up_bias, down_weight, down_bias)))
    stream = layer_input.astype(jnp.float32).reshape(WINDOWS * WIN, D)
    result, pull = jax.vjp(forward_all, stream, params)
    window_ids = jnp.arange(WINDOWS, dtype=jnp.int32)
    owner = window_ids // SLOTS
    valid = window_ids % SLOTS < window_count[owner]
    weights = sample_weight.astype(jnp.float32) * valid.astype(jnp.float32)
    grad_top = (cotangent.astype(jnp.float32) * weights[:, None, None]).reshape(WINDOWS * WIN, D)
    grad_stream, grads = pull(grad_top)
    layer_out = result.reshape(WINDOWS, WIN, D).astype(jnp.bfloat16)
    input_grad = grad_stream.reshape(WINDOWS, WIN, D)
    return (layer_out, input_grad, grads[0], grads[1], grads[2], grads[3], grads[4], grads[5], grads[6], grads[7], grads[8], grads[9], grads[10], grads[11])
```

```python
import functools
import math

import jax
import jax.numpy as jnp
from jax import lax
from jax.experimental import pallas as pl
from jax.experimental.pallas import tpu as pltpu
from jax.sharding import PartitionSpec as P

norm_eps = 1e-05
lane = 128
ones_rows = 16
group_size = 8
log2_e = 1.4426950408889634
far_below = -1e30
bf16 = jnp.bfloat16
f32 = jnp.float32


def nn(left, right):
    return lax.dot_general(left, right, (((1,), (0,)), ((), ())), preferred_element_type=f32)


def nt(left, right):
    return lax.dot_general(left, right, (((1,), (1,)), ((), ())), preferred_element_type=f32)


def nt_split(left, right):
    high = right.astype(bf16)
    return nt(left, high) + nt(left, (right - high.astype(f32)).astype(bf16))


def wide(column, width):
    return jnp.concatenate([column] * (width // lane), axis=1)


def gelu_parts(pre):
    cdf = 0.5 * lax.erf(pre * math.sqrt(0.5)) + 0.5
    bell = jnp.exp2((pre * pre) * (-0.5 * log2_e) + math.log2(1.0 / math.sqrt(2.0 * math.pi)))
    return pre * cdf, cdf + pre * bell


def eye(size):
    rows = lax.broadcasted_iota(jnp.int32, (size, size), 0)
    cols = lax.broadcasted_iota(jnp.int32, (size, size), 1)
    return (rows == cols).astype(f32).astype(bf16)


def side_by_side(works, between={}):
    works = [work for work in works if work is not None]
    turn = 0
    while works:
        if turn in between:
            between[turn]()
        works = [work for work in works if next(work, work) is None]
        turn += 1


def fold(block, act):
    rows = [block[i : i + 8] for i in range(0, block.shape[0], 8)]
    return functools.reduce(act, rows)


def spread_rows(block, h, heads):
    size, toks = block.shape
    parts = []
    if h:
        parts.append(jnp.zeros((h * size, toks), block.dtype))
    parts.append(block)
    if h < heads - 1:
        parts.append(jnp.zeros(((heads - 1 - h) * size, toks), block.dtype))
    return jnp.concatenate(parts, axis=0)


class Sizes:
    def __init__(self, slots, win, width, layers, units, heads, groups):
        self.slots, self.win, self.width = slots, win, width
        self.layers, self.units, self.heads, self.groups = layers, units, heads, groups
        self.hd = width // heads
        self.share = units // heads
        self.toks = -(-win // lane) * lane
        self.own = slots // heads
        self.block = 16 if self.own < 16 else self.own
        self.upper_rows = 3 * self.hd + self.hd + width + self.share
        self.first_rows = self.hd + width + self.share
        step = 16 * groups
        round_up = lambda rows: -(-rows // step) * step
        self.early = [
            (self.first_rows, (), round_up(self.first_rows))
            if l == 0
            else (self.upper_rows, (self.first_rows,), round_up(self.upper_rows))
            for l in range(layers)
        ]
        self.late_vec = 3 * self.hd
        self.vec = 16 * -(-8 * layers // 16)
        self.late_used = self.late_vec + self.vec
        self.late = round_up(self.late_used)

    def key(self):
        return (self.slots, self.win, self.width, self.layers, self.units, self.heads, self.groups)


class Reduction:
    def __init__(self, sizes, rows, used, cuts, done, refs):
        self.sizes, self.rows, self.used = sizes, rows, used
        self.chunk = rows // sizes.groups
        (
            self.out_buf,
            self.head_in,
            self.mid,
            self.dp_in,
            self.total,
            self.head_send,
            self.head_recv,
            self.dp_send,
            self.dp_recv,
            self.all_send,
            self.all_recv,
            self.own_sem,
        ) = refs
        self.done = done
        self.cuts = [0] + list(cuts) + [used]
        self.me = lax.axis_index("head")
        self.group = lax.axis_index("dp")

    @staticmethod
    def scratch(sizes, rows, used, width, parts):
        chunk = rows // sizes.groups
        vm = pltpu.VMEM
        dma = pltpu.SemaphoreType.DMA
        return [
            vm((sizes.heads, used, width), bf16),
            vm((sizes.heads - 1, used, width), bf16),
            vm((rows, width), bf16),
            vm((sizes.groups - 1, chunk, width), bf16),
            vm((chunk, width), bf16),
            dma((parts, sizes.heads - 1)),
            dma((parts, sizes.heads - 1)),
            dma((sizes.groups - 1,)),
            dma((sizes.groups - 1,)),
            dma((sizes.groups - 1,)),
            dma((sizes.groups - 1,)),
            dma((1,)),
        ]

    def head_copy(self, k, i):
        peer = lax.rem(self.me + k, self.sizes.heads)
        span = pl.ds(self.cuts[i], self.cuts[i + 1] - self.cuts[i])
        return pltpu.make_async_remote_copy(
            src_ref=self.out_buf.at[peer, span],
            dst_ref=self.head_in.at[k - 1, span],
            send_sem=self.head_send.at[i, k - 1],
            recv_sem=self.head_recv.at[i, k - 1],
            device_id={"head": peer},
            device_id_type=pl.DeviceIdType.MESH,
        )

    def part(self, index):
        return pl.ds(pl.multiple_of(index * self.chunk, 16), self.chunk)

    def dp_copy(self, k):
        peer = lax.rem(self.group + k, self.sizes.groups)
        return pltpu.make_async_remote_copy(
            src_ref=self.mid.at[self.part(peer)],
            dst_ref=self.dp_in.at[k - 1],
            send_sem=self.dp_send.at[k - 1],
            recv_sem=self.dp_recv.at[k - 1],
            device_id={"dp": peer},
            device_id_type=pl.DeviceIdType.MESH,
        )

    def all_copy(self, k):
        peer = lax.rem(self.group + k, self.sizes.groups)
        return pltpu.make_async_remote_copy(
            src_ref=self.total,
            dst_ref=self.done.at[self.part(self.group)],
            send_sem=self.all_send.at[k - 1],
            recv_sem=self.all_recv.at[k - 1],
            device_id={"dp": peer},
            device_id_type=pl.DeviceIdType.MESH,
        )

    def start_heads(self, i):
        for k in range(1, self.sizes.heads):
            self.head_copy(k, i).start()

    def start_groups(self):
        for i in range(len(self.cuts) - 1):
            for k in range(1, self.sizes.heads):
                self.head_copy(k, i).wait()
        total = self.out_buf[self.me].astype(f32)
        for k in range(1, self.sizes.heads):
            total += self.head_in[k - 1].astype(f32)
        self.mid[: self.used] = total.astype(bf16)
        each_peer(self.sizes.groups, lambda k: self.dp_copy(k).start())

    def start_gather(self):
        each_peer(self.sizes.groups, lambda k: self.dp_copy(k).wait())
        own = self.part(self.group)
        total = self.mid[own].astype(f32)
        for k in range(1, self.sizes.groups):
            total += self.dp_in[k - 1].astype(f32)
        self.total[...] = total.astype(bf16)
        self.own_copy().start()
        each_peer(self.sizes.groups, lambda k: self.all_copy(k).start())

    def own_copy(self):
        return pltpu.make_async_copy(
            self.total, self.done.at[self.part(self.group)], self.own_sem.at[0]
        )

    def finish(self):
        self.own_copy().wait()
        each_peer(self.sizes.groups, lambda k: self.all_copy(k).wait())


def each_peer(count, act):
    def step(k, carry):
        act(k)
        return carry

    if count <= 8:
        for k in range(1, count):
            act(k)
    else:
        lax.fori_loop(1, count, step, 0)


def body(sizes, *refs):
    inputs = 18
    early_refs = refs[inputs : inputs + sizes.layers]
    exchange(sizes, early_refs, *refs[:inputs], *refs[inputs + sizes.layers :])


def exchange(
    sizes,
    early_refs,
    count_ref,
    sample_ref,
    x_ref,
    cot_ref,
    qkv_shard_ref,
    qv_ref,
    out_w_ref,
    up_w_ref,
    down_w_ref,
    g1_ref,
    b1_ref,
    bo_ref,
    g2_ref,
    b2_ref,
    bd_ref,
    bu_ref,
    lo_ref,
    ig_ref,
    late_ref,
    stream,
    xh1,
    rs1,
    n1e,
    qkv,
    v_tok,
    probs,
    inv,
    att,
    xh2,
    rs2,
    n2e,
    act,
    slope,
    qkv_t_ref,
    qkv_n,
    out_t,
    up_t,
    down_t,
    cols,
    mask,
    g_qkv,
    g_out,
    g_up,
    g_down,
    g_vec,
    k_tok,
    g_scr,
    gl_kept,
    gp_kept,
    gm_kept,
    gqkv_kept,
    vec_rows,
    lo_stage,
    ig_stage,
    qv_own,
    qv_all,
    shard_send,
    shard_recv,
    qv_send,
    qv_recv,
    lo_send,
    lo_recv,
    ig_send,
    ig_recv,
    own_sem,
    x_in,
    x_rows,
    cot_t,
    in_sem,
    *reduction_refs,
):
    layers, heads, width, units = sizes.layers, sizes.heads, sizes.width, sizes.units
    win, toks, own, hd, share = sizes.win, sizes.toks, sizes.own, sizes.hd, sizes.share
    scale = 1.0 / math.sqrt(hd)
    half = toks // 2
    abreast = math.gcd(own, group_size)
    me = lax.axis_index("head")
    group = lax.axis_index("dp")
    earlies = [
        Reduction(sizes, rows, used, cuts, early_refs[l], reduction_refs[12 * l : 12 * (l + 1)])
        for l, (used, cuts, rows) in enumerate(sizes.early)
    ]
    late = Reduction(sizes, sizes.late, sizes.late_used, (), late_ref, reduction_refs[12 * layers :])

    def head_peer(k):
        return lax.rem(me + k, heads)

    first = me * own
    fetch_from = pl.multiple_of(first // sizes.block * sizes.block, 16)
    fetches = [
        pltpu.make_async_copy(src.at[:, pl.ds(fetch_from, sizes.block)], dst, in_sem.at[i])
        for i, (src, dst) in enumerate(((x_ref, x_in), (cot_ref, x_in)))
    ]
    fetches[0].start()
    barrier = pltpu.get_barrier_semaphore()
    for k in range(1, heads):
        pl.semaphore_signal(
            barrier, inc=1, device_id={"head": head_peer(k)}, device_id_type=pl.DeviceIdType.MESH
        )

    def greet(k):
        pl.semaphore_signal(
            barrier,
            inc=1,
            device_id={"dp": lax.rem(group + k, sizes.groups)},
            device_id_type=pl.DeviceIdType.MESH,
        )

    each_peer(sizes.groups, greet)

    c_g1, c_b1, c_qkv, c_bo = 0, width, 2 * width, 5 * width
    c_g2, c_b2, c_bd, c_up = 6 * width, 7 * width, 8 * width, 9 * width

    identity = eye(width)
    identity_tok = eye(toks)

    def row_to_column(row):
        return jnp.transpose(jnp.broadcast_to(row, (lane, lane)))

    qv_own[...] = jnp.zeros_like(qv_own)
    for l in range(layers):
        qv_own[l : l + 1, :hd] = qv_ref[l : l + 1, :hd]
        qv_own[l : l + 1, 2 * hd : 3 * hd] = qv_ref[l : l + 1, hd : 2 * hd]
    mine = pl.ds(pl.multiple_of(me * 3 * hd, 16), 3 * hd)
    own_shard = pltpu.make_async_copy(qkv_shard_ref, qkv_t_ref.at[:, mine], own_sem.at[0])
    own_qv = pltpu.make_async_copy(qv_own, qv_all.at[me], own_sem.at[1])

    def shard_copy(k):
        return pltpu.make_async_remote_copy(
            src_ref=qkv_shard_ref,
            dst_ref=qkv_t_ref.at[:, mine],
            send_sem=shard_send.at[k - 1],
            recv_sem=shard_recv.at[k - 1],
            device_id={"head": head_peer(k)},
            device_id_type=pl.DeviceIdType.MESH,
        )

    def qv_copy(k):
        return pltpu.make_async_remote_copy(
            src_ref=qv_own,
            dst_ref=qv_all.at[me],
            send_sem=qv_send.at[k - 1],
            recv_sem=qv_recv.at[k - 1],
            device_id={"head": head_peer(k)},
            device_id_type=pl.DeviceIdType.MESH,
        )

    pl.semaphore_wait(barrier, heads - 1 + sizes.groups - 1)
    own_shard.start()
    own_qv.start()
    for k in range(1, heads):
        qv_copy(k).start()
        shard_copy(k).start()

    def sort_rows(src, dst):
        step = 10 if win % 10 == 0 else 1
        for t in range(0, win, step):
            block = src[t : t + step].astype(f32)
            rows = block[:, :own]
            for i in range(1, sizes.block // own):
                here = first - fetch_from == i * own
                rows = jnp.where(here, block[:, i * own : (i + 1) * own], rows)
            dst[t * own : (t + step) * own] = rows.reshape(step * own, width)
        dst[win * own :] = jnp.zeros(((toks - win) * own, width), f32)

    def turned(src, w):
        return nt(identity, src[pl.ds(w, toks, stride=own), :].astype(bf16))

    def put_column(l, start, ref):
        cols[l, start : start + width] = row_to_column(ref[l : l + 1, :])

    for l in range(layers):
        out_t[l] = nt(identity, out_w_ref[l]).astype(bf16)
        for part in range(units // width):
            span = slice(part * width, (part + 1) * width)
            up_t[l, span, :] = jnp.transpose(up_w_ref[l, :, span].astype(f32)).astype(bf16)
            cols[l, c_up + part * width : c_up + (part + 1) * width] = row_to_column(
                bu_ref[l : l + 1, span]
            )
        down_t[l] = nt(identity, down_w_ref[l]).astype(bf16)
        for start, ref in (
            (c_bo, bo_ref),
            (c_g2, g2_ref),
            (c_b2, b2_ref),
            (c_bd, bd_ref),
        ):
            put_column(l, start, ref)
        put_column(l, c_g1, g1_ref)
        put_column(l, c_b1, b1_ref)
    key_pos = lax.broadcasted_iota(jnp.int32, (half, half), 0)
    query_pos = lax.broadcasted_iota(jnp.int32, (half, half), 1)
    mask[...] = jnp.where(key_pos <= query_pos, 0.0, far_below)
    g_vec[...] = jnp.zeros_like(g_vec)
    vec_rows[...] = jnp.zeros_like(vec_rows)
    for packet in earlies + [late]:
        if packet.rows > packet.used:
            packet.mid[packet.used :] = jnp.zeros((packet.rows - packet.used, width), bf16)

    for w in range(own):
        for l in range(layers):
            n1e[l, w, width:, :] = jnp.ones((ones_rows, toks), bf16)
            n2e[l, w, width:, :] = jnp.ones((ones_rows, toks), bf16)
            att[l, w, width:, :] = jnp.ones((ones_rows, toks), bf16)
            act[l, w, units:, :] = jnp.ones((ones_rows, toks), bf16)
        for h in range(heads):
            g_scr[w, h, half:, :half] = jnp.zeros((half, half), bf16)
            for l in range(layers):
                probs[l, w, h, half:, :half] = jnp.zeros((half, half), bf16)

    fetches[0].wait()
    sort_rows(x_in, x_rows)
    fetches[1].start()
    for w in range(own):
        stream[w] = turned(x_rows, w)

    fetches[1].wait()
    sort_rows(x_in, x_rows)
    for w in range(own):
        cot_t[w] = turned(x_rows, w).astype(bf16)

    def col(l, start, count):
        return wide(cols[l, start : start + count, :], toks)

    step = hd


    def spans(start, count):
        return [slice(r, r + step) for r in range(start, start + count, step)]

    def norm(w, l, gain, shift, unit_ref, spread_ref, low_ref):
        total = sum(fold(stream[w, r], jnp.add) for r in spans(0, width))
        mean = jnp.sum(total, axis=0, keepdims=True) * (1.0 / width)
        square = 0.0
        for r in spans(0, width):
            center = stream[w, r] - mean
            square += fold(center * center, jnp.add)
        spread = lax.rsqrt(jnp.sum(square, axis=0, keepdims=True) * (1.0 / width) + norm_eps)
        spread_ref[l, w] = spread
        for r in spans(0, width):
            unit = (stream[w, r] - mean) * spread
            unit_ref[l, w, r] = unit
            low_ref[l, w, r] = (
                unit * col(l, gain + r.start, step) + col(l, shift + r.start, step)
            ).astype(bf16)

    for w in range(own):
        norm(w, 0, c_g1, c_b1, xh1, rs1, n1e)
    own_shard.wait()
    own_qv.wait()
    for k in range(1, heads):
        qv_copy(k).wait()
        shard_copy(k).wait()
    for l in range(layers):
        qkv_n[l] = nt(identity, qkv_t_ref[l]).astype(bf16)
        for h in range(heads):
            cols[l, c_qkv + 3 * hd * h : c_qkv + 3 * hd * (h + 1)] = row_to_column(
                qv_all[h, l : l + 1, :]
            )[: 3 * hd]
    def forward(l, w):
        if l:
            norm(w, l, c_g1, c_b1, xh1, rs1, n1e)
            yield
        made = nn(qkv_t_ref[l], n1e[l, w, :width])
        for i, r in enumerate(spans(0, 3 * width)):
            piece = made[r] + col(l, c_qkv + r.start, step)
            qkv[l, w, r] = (piece if i % 3 else piece * (scale * log2_e)).astype(bf16)
        yield
        rows_of = lambda h, which: slice((3 * h + which) * hd, (3 * h + which + 1) * hd)
        kv_all = jnp.concatenate(
            [qkv[l, w, rows_of(h, which)] for which in (1, 2) for h in range(heads)], axis=0
        )
        made = nt(identity_tok, kv_all)
        for r in spans(0, toks):
            k_tok[w, r] = made[r, :width].astype(bf16)
            v_tok[l, w, r] = made[r, width:].astype(bf16)
        for h in range(heads):
            yield
            s = nn(k_tok[w], spread_rows(qkv[l, w, rows_of(h, 0)], h, heads))
            top0 = top1 = None
            for r in spans(0, half):
                far = slice(r.start + half, r.stop + half)
                new0 = fold(s[r, :half] + mask[r], jnp.maximum)
                new1 = jnp.maximum(
                    fold(s[r, half:], jnp.maximum), fold(s[far, half:] + mask[r], jnp.maximum)
                )
                top0 = new0 if top0 is None else jnp.maximum(top0, new0)
                top1 = new1 if top1 is None else jnp.maximum(top1, new1)
            top0 = jnp.max(top0, axis=0, keepdims=True)
            top1 = jnp.max(top1, axis=0, keepdims=True)
            for r in spans(0, half):
                far = slice(r.start + half, r.stop + half)
                probs[l, w, h, r, :half] = jnp.exp2(s[r, :half] + mask[r] - top0).astype(bf16)
                probs[l, w, h, r, half:] = jnp.exp2(s[r, half:] - top1).astype(bf16)
                probs[l, w, h, far, half:] = jnp.exp2(s[far, half:] + mask[r] - top1).astype(bf16)
            yield
            v_ext = jnp.concatenate(
                [qkv[l, w, rows_of(h, 2)], jnp.ones((ones_rows, toks), bf16)], axis=0
            )
            o = nn(v_ext, probs[l, w, h])
            inverse = 1.0 / o[hd : hd + 1]
            inv[l, w, h] = inverse
            att[l, w, hd * h : hd * (h + 1)] = (o[:hd] * inverse).astype(bf16)
        yield
        made = nn(out_t[l], att[l, w, :width])
        for r in spans(0, width):
            stream[w, r] = stream[w, r] + made[r] + col(l, c_bo + r.start, step)
        norm(w, l, c_g2, c_b2, xh2, rs2, n2e)
        yield
        made = nn(up_t[l], n2e[l, w, :width])
        for r in spans(0, units):
            a, sl = gelu_parts(made[r] + col(l, c_up + r.start, step))
            act[l, w, r] = a.astype(bf16)
            slope[l, w, r] = sl.astype(bf16)
        yield
        made = nn(down_t[l], act[l, w, :units])
        for r in spans(0, width):
            value = stream[w, r] + made[r] + col(l, c_bd + r.start, step)
            if l < layers - 1:
                stream[w, r] = value
            else:
                lo_stage[r.start // hd, w] = value.astype(bf16)

    def norm_sums(l, w, grad, gain, unit_ref, which):
        plain = tilted = 0.0
        for r in spans(0, width):
            by_unit = grad[r] * unit_ref[l, w, r]
            at = slice(which * width + r.start, which * width + r.stop)
            g_vec[l, at] += by_unit
            at = slice((which + 1) * width + r.start, (which + 1) * width + r.stop)
            g_vec[l, at] += grad[r]
            column = col(l, gain + r.start, step)
            plain += fold(grad[r] * column, jnp.add)
            tilted += fold(by_unit * column, jnp.add)
        return (
            jnp.sum(plain, axis=0, keepdims=True) * (1.0 / width),
            jnp.sum(tilted, axis=0, keepdims=True) * (1.0 / width),
        )

    def norm_back(l, w, grad, gain, unit_ref, spread_ref, means, emit):
        spread = spread_ref[l, w]
        for r in spans(0, width):
            s = grad[r] * col(l, gain + r.start, step)
            emit(r, stream[w, r] + spread * (s - means[0] - unit_ref[l, w, r] * means[1]))

    def backward_units(l, w):
        if l == layers - 1:
            slot = me * own + w
            weight = jnp.where(slot < count_ref[0], sample_ref[slot], 0.0)
        for r in spans(0, width):
            if l == layers - 1:
                stream[w, r] = cot_t[w, r].astype(f32) * weight
            gl_kept[w, r] = stream[w, r].astype(bf16)
        yield
        made = nn(down_w_ref[l], gl_kept[w])
        for r in spans(0, units):
            gp_kept[w, r] = made[r].astype(bf16) * slope[l, w, r]
        yield
        gn = nn(up_w_ref[l], gp_kept[w])
        yield
        means = norm_sums(l, w, gn, c_g2, xh2, 2)

        def emit(r, value):
            stream[w, r] = value
            gm_kept[w, r] = value.astype(bf16)

        norm_back(l, w, gn, c_g2, xh2, rs2, means, emit)

    def backward_attention(l, w, after):
        ga = nn(out_w_ref[l], gm_kept[w])
        shares, dots = [], []
        for h in range(heads):
            rows = slice(h * hd, (h + 1) * hd)
            gs = (ga[rows] * inv[l, w, h]).astype(bf16)
            shares.append(gs)
            dots.append(
                jnp.sum(gs.astype(f32) * att[l, w, rows, :].astype(f32), axis=0, keepdims=True)
            )
        yield
        for h in range(heads):
            base = 3 * h * hd
            yield
            gs, dot = shares[h], dots[h]
            made = nn(v_tok[l, w], spread_rows(gs, h, heads))
            gqkv_kept[w, base + 2 * hd : base + 3 * hd] = nt(gs, probs[l, w, h]).astype(bf16)
            d0, d1 = dot[:, :half], dot[:, half:]
            for r in spans(0, half):
                far = slice(r.start + half, r.stop + half)
                g_scr[w, h, r, :half] = probs[l, w, h, r, :half] * (made[r, :half] - d0).astype(bf16)
                g_scr[w, h, r, half:] = probs[l, w, h, r, half:] * (made[r, half:] - d1).astype(bf16)
                g_scr[w, h, far, half:] = probs[l, w, h, far, half:] * (
                    made[far, half:] - d1
                ).astype(bf16)
            yield
            q = qkv[l, w, base : base + hd, :]
            k = qkv[l, w, base + hd : base + 2 * hd, :]
            g = g_scr[w, h]
            gq = (nn(k, g) * scale).astype(bf16)
            gk = (nt(q, g) * (1.0 / log2_e)).astype(bf16)
            gqkv_kept[w, base : base + hd] = gq
            gqkv_kept[w, base + hd : base + 2 * hd] = gk
        yield
        gn = nn(qkv_n[l], gqkv_kept[w])
        yield
        means = norm_sums(l, w, gn, c_g1, xh1, 0)
        after(w, gn, means)

    def lanes(ref, ws):
        return jnp.concatenate([ref[w] for w in ws], axis=1)

    def unit_sums(l, ws):
        def add(ref, value):
            ref[l] = value if ws[0] == 0 else ref[l] + value

        add(g_down, nt(lanes(act.at[l], ws), lanes(gl_kept, ws)))
        add(g_up, nt(lanes(n2e.at[l], ws), lanes(gp_kept, ws)))
        add(g_out, nt(lanes(att.at[l], ws), lanes(gm_kept, ws)))

    def qkv_sums(l, ws):
        value = nt(lanes(gqkv_kept, ws), lanes(n1e.at[l], ws))
        g_qkv[l] = value if ws[0] == 0 else g_qkv[l] + value

    def run(step, first, last, width=1):
        def inner(i, carry):
            side_by_side([step(first + i * width + u) for u in range(width)])
            return carry

        if last - first == width:
            inner(0, 0)
        else:
            lax.fori_loop(0, (last - first) // width, inner, 0)

    last = math.gcd(own, 4)
    cut = own - last

    def lo_copy(k):
        peer = head_peer(k)
        return pltpu.make_async_remote_copy(
            src_ref=lo_stage.at[peer],
            dst_ref=lo_ref.at[pl.ds(me * own, own)],
            send_sem=lo_send.at[k - 1],
            recv_sem=lo_recv.at[k - 1],
            device_id={"head": peer},
            device_id_type=pl.DeviceIdType.MESH,
        )

    def ig_copy(k, i):
        peer = head_peer(k)
        return pltpu.make_async_remote_copy(
            src_ref=ig_stage.at[peer, pl.ds(i * last, last)],
            dst_ref=ig_ref.at[pl.ds(me * own + i * last, last)],
            send_sem=ig_send.at[k - 1, i],
            recv_sem=ig_recv.at[k - 1, i],
            device_id={"head": peer},
            device_id_type=pl.DeviceIdType.MESH,
        )

    for l in range(layers):
        run(functools.partial(forward, l), 0, own, abreast)

    own_lo = pltpu.make_async_copy(
        lo_stage.at[me], lo_ref.at[pl.ds(me * own, own)], own_sem.at[2]
    )
    own_lo.start()
    for k in range(1, heads):
        lo_copy(k).start()

    def vector_rows(l, norm_index):
        at = slice(2 * norm_index * width, 2 * (norm_index + 1) * width)
        return nt_split(jnp.ones((16, toks), bf16), g_vec[l, at])

    def qkv_bias_rows(l):
        at = lax.broadcasted_iota(jnp.int32, (16, width + ones_rows), 1)
        return nt_split((at == width).astype(f32).astype(bf16), g_qkv[l])

    def pack_units(l):
        buf = earlies[l].out_buf
        for h in range(heads):
            at = 0
            buf[h, at : at + hd] = g_out[l, hd * h : hd * (h + 1), :].astype(bf16)
            at += hd
            buf[h, at : at + width] = g_up[l, :width, share * h : share * (h + 1)].astype(bf16)
            at += width
            buf[h, at : at + share] = g_down[l, share * h : share * (h + 1), :].astype(bf16)

    def pack_qkv(l):
        r = sizes.first_rows
        for h in range(heads):
            earlies[l].out_buf[h, r : r + 3 * hd] = g_qkv[
                l, 3 * hd * h : 3 * hd * (h + 1), :width
            ].astype(bf16)

    def put_row(at, row):
        for h in range(heads):
            vec_rows[h, at : at + 1] = row

    def put_norm(l, norm_index, at):
        sums = vector_rows(l, norm_index)
        put_row(at, sums[:1, :width])
        put_row(at + 1, sums[:1, width:])

    def put_qkv(l):
        biases = qkv_bias_rows(l)
        for h in range(heads):
            for i in range(3):
                at = (3 * h + i) * hd
                vec_rows[h, 8 * l + 7 : 8 * l + 8, i * hd : (i + 1) * hd] = biases[:1, at : at + hd]

    def pack_vectors():
        for l in range(layers):
            v = 8 * l
            if l:
                put_norm(l, 0, v)
                put_qkv(l)
            put_row(v + 2, g_out[l, width : width + 1, :])
            put_norm(l, 1, v + 3)
            put_row(v + 5, g_down[l, units : units + 1, :])
            for h in range(heads):
                vec_rows[h, v + 6 : v + 7] = g_up[
                    l, width : width + 1, share * h : share * (h + 1)
                ]

    def pack_late():
        put_norm(0, 0, 0)
        put_qkv(0)
        for h in range(heads):
            late.out_buf[h, : 3 * hd] = g_qkv[0, 3 * hd * h : 3 * hd * (h + 1), :width].astype(
                bf16
            )
            late.out_buf[h, 3 * hd :] = vec_rows[h].astype(bf16)

    def give(w, gn, means):
        def emit(r, value):
            ig_stage[r.start // hd, w] = value.astype(bf16)

        norm_back(0, w, gn, c_g1, xh1, rs1, means, emit)
    waiting = {}

    def keep(w, gn, means):
        for i in range(toks // lane):
            at = (w * (toks // lane) + i) * width
            x_rows[at : at + width] = gn[:, i * lane : (i + 1) * lane]
        waiting[w] = means

    everyone = list(range(own))
    for l in range(layers - 1, -1, -1):
        run(functools.partial(backward_units, l), 0, own, abreast)
        steps = {}
        if l < layers - 1:
            steps[heads + 2] = earlies[l + 1].start_gather
        if l:

            def settle(w, gn, means, l=l):
                def emit(r, value):
                    stream[w, r] = value

                norm_back(l, w, gn, c_g1, xh1, rs1, means, emit)

            def unit_step(l=l):
                unit_sums(l, everyone)
                pack_units(l)
                earlies[l].start_heads(0)

            steps[heads] = unit_step
        else:
            settle = keep
            unit_sums(l, everyone)
            pack_units(l)
            earlies[l].start_heads(0)
            steps[2] = pack_vectors
            steps[2 * heads] = earlies[l].start_groups
        if l < layers - 1:
            earlies[l + 1].start_groups()
        side_by_side([backward_attention(l, w, after=settle) for w in everyone], steps)
        if l:
            qkv_sums(l, everyone)
            pack_qkv(l)
            earlies[l].start_heads(1)

    qkv_sums(0, everyone)
    pack_late()
    late.start_heads(0)
    earlies[0].start_gather()
    batches = own // last

    def give_batch(i):
        for w in everyone[i * last : (i + 1) * last]:
            at = w * (toks // lane) * width
            halves = [x_rows[at + i * width : at + (i + 1) * width] for i in range(toks // lane)]
            give(w, jnp.concatenate(halves, axis=1), waiting[w])

    def send_batch(i):
        for k in range(1, heads):
            ig_copy(k, i).start()

    for i in range(batches - 1):
        give_batch(i)
        send_batch(i)
    give_batch(batches - 1)
    own_ig = pltpu.make_async_copy(
        ig_stage.at[me], ig_ref.at[pl.ds(me * own, own)], own_sem.at[3]
    )
    late.start_groups()
    send_batch(batches - 1)
    own_ig.start()
    own_lo.wait()
    for k in range(1, heads):
        lo_copy(k).wait()
    late.start_gather()
    for packet in earlies:
        packet.finish()
    for i in range(batches):
        for k in range(1, heads):
            ig_copy(k, i).wait()
    own_ig.wait()
    late.finish()


def finish_body(sizes, lo_in, ig_in, *refs):
    packets = refs[: sizes.layers + 1]
    write_outputs(sizes, lo_in, ig_in, packets[:-1], packets[-1], *refs[sizes.layers + 1 :])


def write_outputs(
    sizes,
    lo_in,
    ig_in,
    earlies_in,
    late_in,
    lo_out,
    ig_out,
    ln1_g,
    ln1_s,
    qkv_g,
    qv_g,
    out_g,
    out_b,
    ln2_g,
    ln2_s,
    up_g,
    up_b,
    down_g,
    down_b,
):
    hd, width, share = sizes.hd, sizes.width, sizes.share
    lo_out[...] = lo_in[...][:, :, : sizes.win]
    ig_out[...] = ig_in[...][:, :, : sizes.win].astype(f32)
    for l in range(sizes.layers):
        at = 0
        early_in = earlies_in[l]
        out_g[l] = early_in[at : at + hd].astype(f32)
        at += hd
        up_g[l] = early_in[at : at + width].astype(f32)
        at += width
        down_g[l] = early_in[at : at + share].astype(f32)
        at += share
        if l:
            qkv_g[l] = early_in[at : at + 3 * hd].astype(f32)
            at += 3 * hd
        else:
            qkv_g[l] = late_in[: 3 * hd].astype(f32)
    vec = late_in[3 * hd : 3 * hd + sizes.vec].astype(f32)
    for l in range(sizes.layers):
        v = 8 * l
        row = slice(l, l + 1)
        ln1_g[row] = vec[v : v + 1]
        ln1_s[row] = vec[v + 1 : v + 2]
        out_b[row] = vec[v + 2 : v + 3]
        ln2_g[row] = vec[v + 3 : v + 4]
        ln2_s[row] = vec[v + 4 : v + 5]
        down_b[row] = vec[v + 5 : v + 6]
        up_b[row] = vec[v + 6 : v + 7]
        qv = vec[v + 7 : v + 8]
        qv_g[row, :hd] = qv[:, :hd]
        qv_g[row, hd:] = qv[:, 2 * hd : 3 * hd]


def exchange_pass(sizes, count, sample, x, cot, shard, qv, big, small):
    layers, heads, width, units = sizes.layers, sizes.heads, sizes.width, sizes.units
    own, toks, hd, win = sizes.own, sizes.toks, sizes.hd, sizes.win
    vm = lambda *shape: pltpu.VMEM(shape[:-1], shape[-1])
    dma = pltpu.SemaphoreType.DMA
    whole = pl.BlockSpec(memory_space=pltpu.VMEM)
    scalars = pl.BlockSpec(memory_space=pltpu.SMEM)
    left = pl.BlockSpec(memory_space=pl.ANY)
    return pl.pallas_call(
        functools.partial(body, sizes),
        out_shape=(
            jax.ShapeDtypeStruct((sizes.slots, hd, toks), bf16),
            jax.ShapeDtypeStruct((sizes.slots, hd, toks), bf16),
            *[jax.ShapeDtypeStruct((rows, width), bf16) for _, _, rows in sizes.early],
            jax.ShapeDtypeStruct((sizes.late, width), bf16),
        ),
        in_specs=[scalars, scalars, left, left] + [whole] * 12,
        out_specs=(left,) * (layers + 3),
        scratch_shapes=[
            vm(own, width, toks, f32),
            vm(layers, own, width, toks, f32),
            vm(layers, own, 1, toks, f32),
            vm(layers, own, width + ones_rows, toks, bf16),
            vm(layers, own, 3 * width, toks, bf16),
            vm(layers, own, toks, width, bf16),
            vm(layers, own, heads, toks, toks, bf16),
            vm(layers, own, heads, 1, toks, f32),
            vm(layers, own, width + ones_rows, toks, bf16),
            vm(layers, own, width, toks, f32),
            vm(layers, own, 1, toks, f32),
            vm(layers, own, width + ones_rows, toks, bf16),
            vm(layers, own, units + ones_rows, toks, bf16),
            vm(layers, own, units, toks, bf16),
            vm(layers, 3 * width, width, bf16),
            vm(layers, width, 3 * width, bf16),
            vm(layers, width, width, bf16),
            vm(layers, units, width, bf16),
            vm(layers, width, units, bf16),
            vm(layers, 9 * width + units, lane, f32),
            vm(toks // 2, toks // 2, f32),
            vm(layers, 3 * width, width + ones_rows, f32),
            vm(layers, width + ones_rows, width, f32),
            vm(layers, width + ones_rows, units, f32),
            vm(layers, units + ones_rows, width, f32),
            vm(layers, 4 * width, toks, f32),
            vm(own, toks, width, bf16),
            vm(own, heads, toks, toks, bf16),
            vm(own, width, toks, bf16),
            vm(own, units, toks, bf16),
            vm(own, width, toks, bf16),
            vm(own, 3 * width, toks, bf16),
            vm(heads, sizes.vec, width, f32),
            vm(heads, own, hd, toks, bf16),
            vm(heads, own, hd, toks, bf16),
            vm(8, lane, f32),
            vm(heads, 8, lane, f32),
            dma((heads - 1,)),
            dma((heads - 1,)),
            dma((heads - 1,)),
            dma((heads - 1,)),
            dma((heads - 1,)),
            dma((heads - 1,)),
            dma((heads - 1, own)),
            dma((heads - 1, own)),
            dma((4,)),
            vm(win, sizes.block, width, bf16),
            vm(toks * own, width, f32),
            vm(own, width, toks, bf16),
            dma((2,)),
        ]
        + [
            ref
            for used, cuts, rows in sizes.early
            for ref in Reduction.scratch(sizes, rows, used, width, len(cuts) + 1)
        ]
        + Reduction.scratch(sizes, sizes.late, sizes.late_used, width, 1),
        compiler_params=pltpu.CompilerParams(
            vmem_limit_bytes=63 * 1024 * 1024, collective_id=0, has_side_effects=True
        ),
    )(count, sample, x, cot, shard, qv, *big, *small)


def finish_pass(sizes, lo, ig, *packets):
    layers, width, hd, share = sizes.layers, sizes.width, sizes.hd, sizes.share
    whole = pl.BlockSpec(memory_space=pltpu.VMEM)
    out = lambda *shape: jax.ShapeDtypeStruct(shape, f32)
    row = out(layers, width)
    final = (sizes.slots, hd, sizes.win)
    return pl.pallas_call(
        functools.partial(finish_body, sizes),
        out_shape=(
            jax.ShapeDtypeStruct(final, bf16),
            out(*final),
            row,
            row,
            out(layers, 3 * hd, width),
            out(layers, 2 * hd),
            out(layers, hd, width),
            row,
            row,
            row,
            out(layers, width, share),
            out(layers, share),
            out(layers, share, width),
            row,
        ),
        in_specs=[whole] * (2 + len(packets)),
        out_specs=(whole,) * 14,
        compiler_params=pltpu.CompilerParams(vmem_limit_bytes=60 * 1024 * 1024),
    )(lo, ig, *packets)


def shards(
    layer_input,
    cotangent,
    window_count,
    sample_weight,
    ln1_gain,
    ln1_shift,
    qkv_weight,
    qv_bias,
    out_weight,
    out_bias,
    ln2_gain,
    ln2_shift,
    up_weight,
    up_bias,
    down_weight,
    down_bias,
):
    slots, win, width = layer_input.shape
    layers, _, units = up_weight.shape
    sizes = Sizes(
        slots, win, width, layers, units, lax.axis_size("head"), lax.axis_size("dp")
    )
    lo, ig, *packets = exchange_pass(
        sizes,
        window_count,
        sample_weight,
        jnp.swapaxes(layer_input, 0, 1),
        jnp.swapaxes(cotangent, 0, 1),
        jnp.swapaxes(qkv_weight, 1, 2),
        qv_bias,
        (out_weight, up_weight, down_weight),
        (ln1_gain, ln1_shift, out_bias, ln2_gain, ln2_shift, down_bias, up_bias),
    )
    outs = list(finish_pass(sizes, lo, ig, *packets))
    for index in (0, 1, 4):
        outs[index] = jnp.swapaxes(outs[index], 1, 2)
    return tuple(outs)


def solution(mesh):
    return jax.shard_map(
        shards,
        mesh=mesh,
        in_specs=(
            P("dp", None, None),
            P("dp", None, None),
            P("dp"),
            P("dp"),
            P(),
            P(),
            P(None, None, "head"),
            P(None, "head"),
            P(),
            P(),
            P(),
            P(),
            P(),
            P(),
            P(),
            P(),
        ),
        out_specs=(
            P("dp", None, "head"),
            P("dp", None, "head"),
            P(),
            P(),
            P(None, None, "head"),
            P(None, "head"),
            P(None, "head", None),
            P(),
            P(),
            P(),
            P(None, None, "head"),
            P(None, "head"),
            P(None, "head", None),
            P(),
        ),
        check_vma=False,
    )
```

```python
import functools
import math

import jax
import jax.numpy as jnp
from jax import lax
from jax.experimental import pallas as pl
from jax.experimental.pallas import tpu as pltpu
from jax.sharding import PartitionSpec as P

norm_eps = 1e-05
lane = 128
ones_rows = 16
group_size = 8
log2_e = 1.4426950408889634
far_below = -1e30
bf16 = jnp.bfloat16
f32 = jnp.float32


def nn(left, right):
    return lax.dot_general(left, right, (((1,), (0,)), ((), ())), preferred_element_type=f32)


def nt(left, right):
    return lax.dot_general(left, right, (((1,), (1,)), ((), ())), preferred_element_type=f32)


def nt_split(left, right):
    high = right.astype(bf16)
    return nt(left, high) + nt(left, (right - high.astype(f32)).astype(bf16))


def wide(column, width):
    return jnp.concatenate([column] * (width // lane), axis=1)


def gelu_parts(pre):
    cdf = 0.5 * lax.erf(pre * math.sqrt(0.5)) + 0.5
    bell = jnp.exp2((pre * pre) * (-0.5 * log2_e) + math.log2(1.0 / math.sqrt(2.0 * math.pi)))
    return pre * cdf, cdf + pre * bell


def eye(size):
    rows = lax.broadcasted_iota(jnp.int32, (size, size), 0)
    cols = lax.broadcasted_iota(jnp.int32, (size, size), 1)
    return (rows == cols).astype(f32).astype(bf16)


def side_by_side(works, between={}):
    works = [work for work in works if work is not None]
    turn = 0
    while works:
        if turn in between:
            between[turn]()
        works = [work for work in works if next(work, work) is None]
        turn += 1


def fold(block, act):
    rows = [block[i : i + 8] for i in range(0, block.shape[0], 8)]
    return functools.reduce(act, rows)


def spread_rows(block, h, heads):
    size, toks = block.shape
    parts = []
    if h:
        parts.append(jnp.zeros((h * size, toks), block.dtype))
    parts.append(block)
    if h < heads - 1:
        parts.append(jnp.zeros(((heads - 1 - h) * size, toks), block.dtype))
    return jnp.concatenate(parts, axis=0)


class Sizes:
    def __init__(self, slots, win, width, layers, units, heads, groups):
        self.slots, self.win, self.width = slots, win, width
        self.layers, self.units, self.heads, self.groups = layers, units, heads, groups
        self.hd = width // heads
        self.share = units // heads
        self.toks = -(-win // lane) * lane
        self.own = slots // heads
        self.block = 16 if self.own < 16 else self.own
        self.upper_rows = 3 * self.hd + self.hd + width + self.share
        self.first_rows = self.hd + width + self.share
        step = 16 * groups
        round_up = lambda rows: -(-rows // step) * step
        self.early = [
            (self.first_rows, (), round_up(self.first_rows))
            if l == 0
            else (self.upper_rows, (self.first_rows,), round_up(self.upper_rows))
            for l in range(layers)
        ]
        self.late_vec = 3 * self.hd
        self.vec = 16 * -(-8 * layers // 16)
        self.late_used = self.late_vec + self.vec
        self.late = round_up(self.late_used)

    def key(self):
        return (self.slots, self.win, self.width, self.layers, self.units, self.heads, self.groups)


class Reduction:
    def __init__(self, sizes, rows, used, cuts, done, refs):
        self.sizes, self.rows, self.used = sizes, rows, used
        self.chunk = rows // sizes.groups
        (
            self.out_buf,
            self.head_in,
            self.mid,
            self.dp_in,
            self.total,
            self.head_send,
            self.head_recv,
            self.dp_send,
            self.dp_recv,
            self.all_send,
            self.all_recv,
            self.own_sem,
        ) = refs
        self.done = done
        self.cuts = [0] + list(cuts) + [used]
        self.me = lax.axis_index("head")
        self.group = lax.axis_index("dp")

    @staticmethod
    def scratch(sizes, rows, used, width, parts):
        chunk = rows // sizes.groups
        vm = pltpu.VMEM
        dma = pltpu.SemaphoreType.DMA
        return [
            vm((sizes.heads, used, width), bf16),
            vm((sizes.heads - 1, used, width), bf16),
            vm((rows, width), bf16),
            vm((sizes.groups - 1, chunk, width), bf16),
            vm((chunk, width), bf16),
            dma((parts, sizes.heads - 1)),
            dma((parts, sizes.heads - 1)),
            dma((sizes.groups - 1,)),
            dma((sizes.groups - 1,)),
            dma((sizes.groups - 1,)),
            dma((sizes.groups - 1,)),
            dma((1,)),
        ]

    def head_copy(self, k, i):
        peer = lax.rem(self.me + k, self.sizes.heads)
        span = pl.ds(self.cuts[i], self.cuts[i + 1] - self.cuts[i])
        return pltpu.make_async_remote_copy(
            src_ref=self.out_buf.at[peer, span],
            dst_ref=self.head_in.at[k - 1, span],
            send_sem=self.head_send.at[i, k - 1],
            recv_sem=self.head_recv.at[i, k - 1],
            device_id={"head": peer},
            device_id_type=pl.DeviceIdType.MESH,
        )

    def part(self, index):
        return pl.ds(pl.multiple_of(index * self.chunk, 16), self.chunk)

    def dp_copy(self, k):
        peer = lax.rem(self.group + k, self.sizes.groups)
        return pltpu.make_async_remote_copy(
            src_ref=self.mid.at[self.part(peer)],
            dst_ref=self.dp_in.at[k - 1],
            send_sem=self.dp_send.at[k - 1],
            recv_sem=self.dp_recv.at[k - 1],
            device_id={"dp": peer},
            device_id_type=pl.DeviceIdType.MESH,
        )

    def all_copy(self, k):
        peer = lax.rem(self.group + k, self.sizes.groups)
        return pltpu.make_async_remote_copy(
            src_ref=self.total,
            dst_ref=self.done.at[self.part(self.group)],
            send_sem=self.all_send.at[k - 1],
            recv_sem=self.all_recv.at[k - 1],
            device_id={"dp": peer},
            device_id_type=pl.DeviceIdType.MESH,
        )

    def start_heads(self, i):
        for k in range(1, self.sizes.heads):
            self.head_copy(k, i).start()

    def start_groups(self):
        for i in range(len(self.cuts) - 1):
            for k in range(1, self.sizes.heads):
                self.head_copy(k, i).wait()
        total = self.out_buf[self.me].astype(f32)
        for k in range(1, self.sizes.heads):
            total += self.head_in[k - 1].astype(f32)
        self.mid[: self.used] = total.astype(bf16)
        each_peer(self.sizes.groups, lambda k: self.dp_copy(k).start())

    def start_gather(self):
        each_peer(self.sizes.groups, lambda k: self.dp_copy(k).wait())
        own = self.part(self.group)
        total = self.mid[own].astype(f32)
        for k in range(1, self.sizes.groups):
            total += self.dp_in[k - 1].astype(f32)
        self.total[...] = total.astype(bf16)
        self.own_copy().start()
        each_peer(self.sizes.groups, lambda k: self.all_copy(k).start())

    def own_copy(self):
        return pltpu.make_async_copy(
            self.total, self.done.at[self.part(self.group)], self.own_sem.at[0]
        )

    def finish(self):
        self.own_copy().wait()
        each_peer(self.sizes.groups, lambda k: self.all_copy(k).wait())


def each_peer(count, act):
    def step(k, carry):
        act(k)
        return carry

    if count <= 8:
        for k in range(1, count):
            act(k)
    else:
        lax.fori_loop(1, count, step, 0)


def body(sizes, *refs):
    inputs = 18
    early_refs = refs[inputs : inputs + sizes.layers]
    exchange(sizes, early_refs, *refs[:inputs], *refs[inputs + sizes.layers :])


def exchange(
    sizes,
    early_refs,
    count_ref,
    sample_ref,
    x_ref,
    cot_ref,
    qkv_shard_ref,
    qv_ref,
    out_w_ref,
    up_w_ref,
    down_w_ref,
    g1_ref,
    b1_ref,
    bo_ref,
    g2_ref,
    b2_ref,
    bd_ref,
    bu_ref,
    lo_ref,
    ig_ref,
    late_ref,
    stream,
    xh1,
    rs1,
    n1e,
    qkv,
    v_tok,
    probs,
    inv,
    att,
    xh2,
    rs2,
    n2e,
    act,
    slope,
    qkv_t_ref,
    qkv_n,
    out_t,
    up_t,
    down_t,
    cols,
    mask,
    g_qkv,
    g_out,
    g_up,
    g_down,
    g_vec,
    k_tok,
    g_scr,
    gl_kept,
    gp_kept,
    gm_kept,
    gqkv_kept,
    vec_rows,
    lo_stage,
    ig_stage,
    qv_own,
    qv_all,
    shard_send,
    shard_recv,
    qv_send,
    qv_recv,
    lo_send,
    lo_recv,
    ig_send,
    ig_recv,
    own_sem,
    x_in,
    x_rows,
    cot_t,
    in_sem,
    *reduction_refs,
):
    layers, heads, width, units = sizes.layers, sizes.heads, sizes.width, sizes.units
    win, toks, own, hd, share = sizes.win, sizes.toks, sizes.own, sizes.hd, sizes.share
    scale = 1.0 / math.sqrt(hd)
    half = toks // 2
    abreast = math.gcd(own, group_size)
    me = lax.axis_index("head")
    group = lax.axis_index("dp")
    earlies = [
        Reduction(sizes, rows, used, cuts, early_refs[l], reduction_refs[12 * l : 12 * (l + 1)])
        for l, (used, cuts, rows) in enumerate(sizes.early)
    ]
    late = Reduction(sizes, sizes.late, sizes.late_used, (), late_ref, reduction_refs[12 * layers :])

    def head_peer(k):
        return lax.rem(me + k, heads)

    first = me * own
    fetch_from = pl.multiple_of(first // sizes.block * sizes.block, 16)
    fetches = [
        pltpu.make_async_copy(src.at[:, pl.ds(fetch_from, sizes.block)], dst, in_sem.at[i])
        for i, (src, dst) in enumerate(((x_ref, x_in), (cot_ref, x_in)))
    ]
    fetches[0].start()
    barrier = pltpu.get_barrier_semaphore()
    for k in range(1, heads):
        pl.semaphore_signal(
            barrier, inc=1, device_id={"head": head_peer(k)}, device_id_type=pl.DeviceIdType.MESH
        )

    def greet(k):
        pl.semaphore_signal(
            barrier,
            inc=1,
            device_id={"dp": lax.rem(group + k, sizes.groups)},
            device_id_type=pl.DeviceIdType.MESH,
        )

    each_peer(sizes.groups, greet)

    c_g1, c_b1, c_qkv, c_bo = 0, width, 2 * width, 5 * width
    c_g2, c_b2, c_bd, c_up = 6 * width, 7 * width, 8 * width, 9 * width

    identity = eye(width)
    identity_tok = eye(toks)

    def row_to_column(row):
        return jnp.transpose(jnp.broadcast_to(row, (lane, lane)))

    qv_own[...] = jnp.zeros_like(qv_own)
    for l in range(layers):
        qv_own[l : l + 1, :hd] = qv_ref[l : l + 1, :hd]
        qv_own[l : l + 1, 2 * hd : 3 * hd] = qv_ref[l : l + 1, hd : 2 * hd]
    mine = pl.ds(pl.multiple_of(me * 3 * hd, 16), 3 * hd)
    own_shard = pltpu.make_async_copy(qkv_shard_ref, qkv_t_ref.at[:, mine], own_sem.at[0])
    own_qv = pltpu.make_async_copy(qv_own, qv_all.at[me], own_sem.at[1])

    def shard_copy(k):
        return pltpu.make_async_remote_copy(
            src_ref=qkv_shard_ref,
            dst_ref=qkv_t_ref.at[:, mine],
            send_sem=shard_send.at[k - 1],
            recv_sem=shard_recv.at[k - 1],
            device_id={"head": head_peer(k)},
            device_id_type=pl.DeviceIdType.MESH,
        )

    def qv_copy(k):
        return pltpu.make_async_remote_copy(
            src_ref=qv_own,
            dst_ref=qv_all.at[me],
            send_sem=qv_send.at[k - 1],
            recv_sem=qv_recv.at[k - 1],
            device_id={"head": head_peer(k)},
            device_id_type=pl.DeviceIdType.MESH,
        )

    pl.semaphore_wait(barrier, heads - 1 + sizes.groups - 1)
    own_shard.start()
    own_qv.start()
    for k in range(1, heads):
        qv_copy(k).start()
        shard_copy(k).start()

    def sort_rows(src, dst):
        step = 10 if win % 10 == 0 else 1
        for t in range(0, win, step):
            block = src[t : t + step].astype(f32)
            rows = block[:, :own]
            for i in range(1, sizes.block // own):
                here = first - fetch_from == i * own
                rows = jnp.where(here, block[:, i * own : (i + 1) * own], rows)
            dst[t * own : (t + step) * own] = rows.reshape(step * own, width)
        dst[win * own :] = jnp.zeros(((toks - win) * own, width), f32)

    def turned(src, w):
        return nt(identity, src[pl.ds(w, toks, stride=own), :].astype(bf16))

    def put_column(l, start, ref):
        cols[l, start : start + width] = row_to_column(ref[l : l + 1, :])

    for l in range(layers):
        out_t[l] = nt(identity, out_w_ref[l]).astype(bf16)
        for part in range(units // width):
            span = slice(part * width, (part + 1) * width)
            up_t[l, span, :] = jnp.transpose(up_w_ref[l, :, span].astype(f32)).astype(bf16)
            cols[l, c_up + part * width : c_up + (part + 1) * width] = row_to_column(
                bu_ref[l : l + 1, span]
            )
        down_t[l] = nt(identity, down_w_ref[l]).astype(bf16)
        for start, ref in (
            (c_bo, bo_ref),
            (c_g2, g2_ref),
            (c_b2, b2_ref),
            (c_bd, bd_ref),
        ):
            put_column(l, start, ref)
        put_column(l, c_g1, g1_ref)
        put_column(l, c_b1, b1_ref)
    key_pos = lax.broadcasted_iota(jnp.int32, (half, half), 0)
    query_pos = lax.broadcasted_iota(jnp.int32, (half, half), 1)
    mask[...] = jnp.where(key_pos <= query_pos, 0.0, far_below)
    g_vec[...] = jnp.zeros_like(g_vec)
    vec_rows[...] = jnp.zeros_like(vec_rows)
    for packet in earlies + [late]:
        if packet.rows > packet.used:
            packet.mid[packet.used :] = jnp.zeros((packet.rows - packet.used, width), bf16)

    for w in range(own):
        for l in range(layers):
            n1e[l, w, width:, :] = jnp.ones((ones_rows, toks), bf16)
            n2e[l, w, width:, :] = jnp.ones((ones_rows, toks), bf16)
            att[l, w, width:, :] = jnp.ones((ones_rows, toks), bf16)
            act[l, w, units:, :] = jnp.ones((ones_rows, toks), bf16)
        for h in range(heads):
            g_scr[w, h, half:, :half] = jnp.zeros((half, half), bf16)
            for l in range(layers):
                probs[l, w, h, half:, :half] = jnp.zeros((half, half), bf16)

    fetches[0].wait()
    sort_rows(x_in, x_rows)
    fetches[1].start()
    for w in range(own):
        stream[w] = turned(x_rows, w)

    def col(l, start, count):
        return wide(cols[l, start : start + count, :], toks)

    step = hd


    def spans(start, count):
        return [slice(r, r + step) for r in range(start, start + count, step)]

    def norm(w, l, gain, shift, unit_ref, spread_ref, low_ref):
        total = sum(fold(stream[w, r], jnp.add) for r in spans(0, width))
        mean = jnp.sum(total, axis=0, keepdims=True) * (1.0 / width)
        square = 0.0
        for r in spans(0, width):
            center = stream[w, r] - mean
            square += fold(center * center, jnp.add)
        spread = lax.rsqrt(jnp.sum(square, axis=0, keepdims=True) * (1.0 / width) + norm_eps)
        spread_ref[l, w] = spread
        for r in spans(0, width):
            unit = (stream[w, r] - mean) * spread
            unit_ref[l, w, r] = unit
            low_ref[l, w, r] = (
                unit * col(l, gain + r.start, step) + col(l, shift + r.start, step)
            ).astype(bf16)

    for w in range(own):
        norm(w, 0, c_g1, c_b1, xh1, rs1, n1e)
    own_shard.wait()
    own_qv.wait()
    for k in range(1, heads):
        qv_copy(k).wait()
        shard_copy(k).wait()
    for l in range(layers):
        qkv_n[l] = nt(identity, qkv_t_ref[l]).astype(bf16)
        for h in range(heads):
            cols[l, c_qkv + 3 * hd * h : c_qkv + 3 * hd * (h + 1)] = row_to_column(
                qv_all[h, l : l + 1, :]
            )[: 3 * hd]
    fetches[1].wait()
    sort_rows(x_in, x_rows)
    for w in range(own):
        cot_t[w] = turned(x_rows, w).astype(bf16)

    def forward(l, w):
        if l:
            norm(w, l, c_g1, c_b1, xh1, rs1, n1e)
            yield
        made = nn(qkv_t_ref[l], n1e[l, w, :width])
        for i, r in enumerate(spans(0, 3 * width)):
            piece = made[r] + col(l, c_qkv + r.start, step)
            qkv[l, w, r] = (piece if i % 3 else piece * (scale * log2_e)).astype(bf16)
        yield
        rows_of = lambda h, which: slice((3 * h + which) * hd, (3 * h + which + 1) * hd)
        kv_all = jnp.concatenate(
            [qkv[l, w, rows_of(h, which)] for which in (1, 2) for h in range(heads)], axis=0
        )
        made = nt(identity_tok, kv_all)
        for r in spans(0, toks):
            k_tok[w, r] = made[r, :width].astype(bf16)
            v_tok[l, w, r] = made[r, width:].astype(bf16)
        for h in range(heads):
            yield
            s = nn(k_tok[w], spread_rows(qkv[l, w, rows_of(h, 0)], h, heads))
            top0 = top1 = None
            for r in spans(0, half):
                far = slice(r.start + half, r.stop + half)
                new0 = fold(s[r, :half] + mask[r], jnp.maximum)
                new1 = jnp.maximum(
                    fold(s[r, half:], jnp.maximum), fold(s[far, half:] + mask[r], jnp.maximum)
                )
                top0 = new0 if top0 is None else jnp.maximum(top0, new0)
                top1 = new1 if top1 is None else jnp.maximum(top1, new1)
            top0 = jnp.max(top0, axis=0, keepdims=True)
            top1 = jnp.max(top1, axis=0, keepdims=True)
            for r in spans(0, half):
                far = slice(r.start + half, r.stop + half)
                probs[l, w, h, r, :half] = jnp.exp2(s[r, :half] + mask[r] - top0).astype(bf16)
                probs[l, w, h, r, half:] = jnp.exp2(s[r, half:] - top1).astype(bf16)
                probs[l, w, h, far, half:] = jnp.exp2(s[far, half:] + mask[r] - top1).astype(bf16)
            yield
            v_ext = jnp.concatenate(
                [qkv[l, w, rows_of(h, 2)], jnp.ones((ones_rows, toks), bf16)], axis=0
            )
            o = nn(v_ext, probs[l, w, h])
            inverse = 1.0 / o[hd : hd + 1]
            inv[l, w, h] = inverse
            att[l, w, hd * h : hd * (h + 1)] = (o[:hd] * inverse).astype(bf16)
        yield
        made = nn(out_t[l], att[l, w, :width])
        for r in spans(0, width):
            stream[w, r] = stream[w, r] + made[r] + col(l, c_bo + r.start, step)
        norm(w, l, c_g2, c_b2, xh2, rs2, n2e)
        yield
        made = nn(up_t[l], n2e[l, w, :width])
        for r in spans(0, units):
            a, sl = gelu_parts(made[r] + col(l, c_up + r.start, step))
            act[l, w, r] = a.astype(bf16)
            slope[l, w, r] = sl.astype(bf16)
        yield
        made = nn(down_t[l], act[l, w, :units])
        for r in spans(0, width):
            value = stream[w, r] + made[r] + col(l, c_bd + r.start, step)
            if l < layers - 1:
                stream[w, r] = value
            else:
                lo_stage[r.start // hd, w] = value.astype(bf16)

    def norm_sums(l, w, grad, gain, unit_ref, which):
        plain = tilted = 0.0
        for r in spans(0, width):
            by_unit = grad[r] * unit_ref[l, w, r]
            at = slice(which * width + r.start, which * width + r.stop)
            g_vec[l, at] += by_unit
            at = slice((which + 1) * width + r.start, (which + 1) * width + r.stop)
            g_vec[l, at] += grad[r]
            column = col(l, gain + r.start, step)
            plain += fold(grad[r] * column, jnp.add)
            tilted += fold(by_unit * column, jnp.add)
        return (
            jnp.sum(plain, axis=0, keepdims=True) * (1.0 / width),
            jnp.sum(tilted, axis=0, keepdims=True) * (1.0 / width),
        )

    def norm_back(l, w, grad, gain, unit_ref, spread_ref, means, emit):
        spread = spread_ref[l, w]
        for r in spans(0, width):
            s = grad[r] * col(l, gain + r.start, step)
            emit(r, stream[w, r] + spread * (s - means[0] - unit_ref[l, w, r] * means[1]))

    def backward_units(l, w):
        if l == layers - 1:
            slot = me * own + w
            weight = jnp.where(slot < count_ref[0], sample_ref[slot], 0.0)
        for r in spans(0, width):
            if l == layers - 1:
                stream[w, r] = cot_t[w, r].astype(f32) * weight
            gl_kept[w, r] = stream[w, r].astype(bf16)
        yield
        made = nn(down_w_ref[l], gl_kept[w])
        for r in spans(0, units):
            gp_kept[w, r] = made[r].astype(bf16) * slope[l, w, r]
        yield
        gn = nn(up_w_ref[l], gp_kept[w])
        yield
        means = norm_sums(l, w, gn, c_g2, xh2, 2)

        def emit(r, value):
            stream[w, r] = value
            gm_kept[w, r] = value.astype(bf16)

        norm_back(l, w, gn, c_g2, xh2, rs2, means, emit)

    def backward_attention(l, w, after):
        ga = nn(out_w_ref[l], gm_kept[w])
        shares, dots = [], []
        for h in range(heads):
            rows = slice(h * hd, (h + 1) * hd)
            gs = (ga[rows] * inv[l, w, h]).astype(bf16)
            shares.append(gs)
            dots.append(
                jnp.sum(gs.astype(f32) * att[l, w, rows, :].astype(f32), axis=0, keepdims=True)
            )
        yield
        for h in range(heads):
            base = 3 * h * hd
            yield
            gs, dot = shares[h], dots[h]
            made = nn(v_tok[l, w], spread_rows(gs, h, heads))
            gqkv_kept[w, base + 2 * hd : base + 3 * hd] = nt(gs, probs[l, w, h]).astype(bf16)
            d0, d1 = dot[:, :half], dot[:, half:]
            for r in spans(0, half):
                far = slice(r.start + half, r.stop + half)
                g_scr[w, h, r, :half] = probs[l, w, h, r, :half] * (made[r, :half] - d0).astype(bf16)
                g_scr[w, h, r, half:] = probs[l, w, h, r, half:] * (made[r, half:] - d1).astype(bf16)
                g_scr[w, h, far, half:] = probs[l, w, h, far, half:] * (
                    made[far, half:] - d1
                ).astype(bf16)
            yield
            q = qkv[l, w, base : base + hd, :]
            k = qkv[l, w, base + hd : base + 2 * hd, :]
            g = g_scr[w, h]
            gq = (nn(k, g) * scale).astype(bf16)
            gk = (nt(q, g) * (1.0 / log2_e)).astype(bf16)
            gqkv_kept[w, base : base + hd] = gq
            gqkv_kept[w, base + hd : base + 2 * hd] = gk
        yield
        gn = nn(qkv_n[l], gqkv_kept[w])
        yield
        means = norm_sums(l, w, gn, c_g1, xh1, 0)
        after(w, gn, means)

    def lanes(ref, ws):
        return jnp.concatenate([ref[w] for w in ws], axis=1)

    def unit_sums(l, ws):
        def add(ref, value):
            ref[l] = value if ws[0] == 0 else ref[l] + value

        add(g_down, nt(lanes(act.at[l], ws), lanes(gl_kept, ws)))
        add(g_up, nt(lanes(n2e.at[l], ws), lanes(gp_kept, ws)))
        add(g_out, nt(lanes(att.at[l], ws), lanes(gm_kept, ws)))

    def qkv_sums(l, ws):
        value = nt(lanes(gqkv_kept, ws), lanes(n1e.at[l], ws))
        g_qkv[l] = value if ws[0] == 0 else g_qkv[l] + value

    def run(step, first, last, width=1):
        def inner(i, carry):
            side_by_side([step(first + i * width + u) for u in range(width)])
            return carry

        if last - first == width:
            inner(0, 0)
        else:
            lax.fori_loop(0, (last - first) // width, inner, 0)

    last = math.gcd(own, 4)
    cut = own - last

    def lo_copy(k):
        peer = head_peer(k)
        return pltpu.make_async_remote_copy(
            src_ref=lo_stage.at[peer],
            dst_ref=lo_ref.at[pl.ds(me * own, own)],
            send_sem=lo_send.at[k - 1],
            recv_sem=lo_recv.at[k - 1],
            device_id={"head": peer},
            device_id_type=pl.DeviceIdType.MESH,
        )

    def ig_copy(k, i):
        peer = head_peer(k)
        return pltpu.make_async_remote_copy(
            src_ref=ig_stage.at[peer, pl.ds(i * last, last)],
            dst_ref=ig_ref.at[pl.ds(me * own + i * last, last)],
            send_sem=ig_send.at[k - 1, i],
            recv_sem=ig_recv.at[k - 1, i],
            device_id={"head": peer},
            device_id_type=pl.DeviceIdType.MESH,
        )

    for l in range(layers):
        run(functools.partial(forward, l), 0, own, abreast)

    own_lo = pltpu.make_async_copy(
        lo_stage.at[me], lo_ref.at[pl.ds(me * own, own)], own_sem.at[2]
    )
    own_lo.start()
    for k in range(1, heads):
        lo_copy(k).start()

    def vector_rows(l, norm_index):
        at = slice(2 * norm_index * width, 2 * (norm_index + 1) * width)
        return nt_split(jnp.ones((16, toks), bf16), g_vec[l, at])

    def qkv_bias_rows(l):
        at = lax.broadcasted_iota(jnp.int32, (16, width + ones_rows), 1)
        return nt_split((at == width).astype(f32).astype(bf16), g_qkv[l])

    def pack_units(l):
        buf = earlies[l].out_buf
        for h in range(heads):
            at = 0
            buf[h, at : at + hd] = g_out[l, hd * h : hd * (h + 1), :].astype(bf16)
            at += hd
            buf[h, at : at + width] = g_up[l, :width, share * h : share * (h + 1)].astype(bf16)
            at += width
            buf[h, at : at + share] = g_down[l, share * h : share * (h + 1), :].astype(bf16)

    def pack_qkv(l):
        r = sizes.first_rows
        for h in range(heads):
            earlies[l].out_buf[h, r : r + 3 * hd] = g_qkv[
                l, 3 * hd * h : 3 * hd * (h + 1), :width
            ].astype(bf16)

    def put_row(at, row):
        for h in range(heads):
            vec_rows[h, at : at + 1] = row

    def put_norm(l, norm_index, at):
        sums = vector_rows(l, norm_index)
        put_row(at, sums[:1, :width])
        put_row(at + 1, sums[:1, width:])

    def put_qkv(l):
        biases = qkv_bias_rows(l)
        for h in range(heads):
            for i in range(3):
                at = (3 * h + i) * hd
                vec_rows[h, 8 * l + 7 : 8 * l + 8, i * hd : (i + 1) * hd] = biases[:1, at : at + hd]

    def pack_vectors():
        for l in range(layers):
            v = 8 * l
            if l:
                put_norm(l, 0, v)
                put_qkv(l)
            put_row(v + 2, g_out[l, width : width + 1, :])
            put_norm(l, 1, v + 3)
            put_row(v + 5, g_down[l, units : units + 1, :])
            for h in range(heads):
                vec_rows[h, v + 6 : v + 7] = g_up[
                    l, width : width + 1, share * h : share * (h + 1)
                ]

    def pack_late():
        put_norm(0, 0, 0)
        put_qkv(0)
        for h in range(heads):
            late.out_buf[h, : 3 * hd] = g_qkv[0, 3 * hd * h : 3 * hd * (h + 1), :width].astype(
                bf16
            )
            late.out_buf[h, 3 * hd :] = vec_rows[h].astype(bf16)

    def give(w, gn, means):
        def emit(r, value):
            ig_stage[r.start // hd, w] = value.astype(bf16)

        norm_back(0, w, gn, c_g1, xh1, rs1, means, emit)
    waiting = {}

    def keep(w, gn, means):
        for i in range(toks // lane):
            at = (w * (toks // lane) + i) * width
            x_rows[at : at + width] = gn[:, i * lane : (i + 1) * lane]
        waiting[w] = means

    everyone = list(range(own))
    for l in range(layers - 1, -1, -1):
        run(functools.partial(backward_units, l), 0, own, abreast)
        steps = {}
        if l < layers - 1:
            steps[heads + 2] = earlies[l + 1].start_gather
        if l:

            def settle(w, gn, means, l=l):
                def emit(r, value):
                    stream[w, r] = value

                norm_back(l, w, gn, c_g1, xh1, rs1, means, emit)

            def unit_step(l=l):
                unit_sums(l, everyone)
                pack_units(l)
                earlies[l].start_heads(0)

            steps[heads] = unit_step
        else:
            settle = keep
            unit_sums(l, everyone)
            pack_units(l)
            earlies[l].start_heads(0)
            steps[2] = pack_vectors
            steps[2 * heads] = earlies[l].start_groups
        if l < layers - 1:
            earlies[l + 1].start_groups()
        side_by_side([backward_attention(l, w, after=settle) for w in everyone], steps)
        if l:
            qkv_sums(l, everyone)
            pack_qkv(l)
            earlies[l].start_heads(1)

    qkv_sums(0, everyone)
    pack_late()
    late.start_heads(0)
    batches = own // last

    def give_batch(i):
        for w in everyone[i * last : (i + 1) * last]:
            at = w * (toks // lane) * width
            halves = [x_rows[at + i * width : at + (i + 1) * width] for i in range(toks // lane)]
            give(w, jnp.concatenate(halves, axis=1), waiting[w])

    def send_batch(i):
        for k in range(1, heads):
            ig_copy(k, i).start()

    for i in range(batches - 1):
        give_batch(i)
        send_batch(i)
    give_batch(batches - 1)
    own_ig = pltpu.make_async_copy(
        ig_stage.at[me], ig_ref.at[pl.ds(me * own, own)], own_sem.at[3]
    )
    late.start_groups()
    earlies[0].start_gather()
    send_batch(batches - 1)
    own_ig.start()
    own_lo.wait()
    for k in range(1, heads):
        lo_copy(k).wait()
    late.start_gather()
    for packet in earlies:
        packet.finish()
    for i in range(batches):
        for k in range(1, heads):
            ig_copy(k, i).wait()
    own_ig.wait()
    late.finish()


def finish_body(sizes, lo_in, ig_in, *refs):
    packets = refs[: sizes.layers + 1]
    write_outputs(sizes, lo_in, ig_in, packets[:-1], packets[-1], *refs[sizes.layers + 1 :])


def write_outputs(
    sizes,
    lo_in,
    ig_in,
    earlies_in,
    late_in,
    lo_out,
    ig_out,
    ln1_g,
    ln1_s,
    qkv_g,
    qv_g,
    out_g,
    out_b,
    ln2_g,
    ln2_s,
    up_g,
    up_b,
    down_g,
    down_b,
):
    hd, width, share = sizes.hd, sizes.width, sizes.share
    lo_out[...] = lo_in[...][:, :, : sizes.win]
    ig_out[...] = ig_in[...][:, :, : sizes.win].astype(f32)
    for l in range(sizes.layers):
        at = 0
        early_in = earlies_in[l]
        out_g[l] = early_in[at : at + hd].astype(f32)
        at += hd
        up_g[l] = early_in[at : at + width].astype(f32)
        at += width
        down_g[l] = early_in[at : at + share].astype(f32)
        at += share
        if l:
            qkv_g[l] = early_in[at : at + 3 * hd].astype(f32)
            at += 3 * hd
        else:
            qkv_g[l] = late_in[: 3 * hd].astype(f32)
    vec = late_in[3 * hd : 3 * hd + sizes.vec].astype(f32)
    for l in range(sizes.layers):
        v = 8 * l
        row = slice(l, l + 1)
        ln1_g[row] = vec[v : v + 1]
        ln1_s[row] = vec[v + 1 : v + 2]
        out_b[row] = vec[v + 2 : v + 3]
        ln2_g[row] = vec[v + 3 : v + 4]
        ln2_s[row] = vec[v + 4 : v + 5]
        down_b[row] = vec[v + 5 : v + 6]
        up_b[row] = vec[v + 6 : v + 7]
        qv = vec[v + 7 : v + 8]
        qv_g[row, :hd] = qv[:, :hd]
        qv_g[row, hd:] = qv[:, 2 * hd : 3 * hd]


def exchange_pass(sizes, count, sample, x, cot, shard, qv, big, small):
    layers, heads, width, units = sizes.layers, sizes.heads, sizes.width, sizes.units
    own, toks, hd, win = sizes.own, sizes.toks, sizes.hd, sizes.win
    vm = lambda *shape: pltpu.VMEM(shape[:-1], shape[-1])
    dma = pltpu.SemaphoreType.DMA
    whole = pl.BlockSpec(memory_space=pltpu.VMEM)
    scalars = pl.BlockSpec(memory_space=pltpu.SMEM)
    left = pl.BlockSpec(memory_space=pl.ANY)
    return pl.pallas_call(
        functools.partial(body, sizes),
        out_shape=(
            jax.ShapeDtypeStruct((sizes.slots, hd, toks), bf16),
            jax.ShapeDtypeStruct((sizes.slots, hd, toks), bf16),
            *[jax.ShapeDtypeStruct((rows, width), bf16) for _, _, rows in sizes.early],
            jax.ShapeDtypeStruct((sizes.late, width), bf16),
        ),
        in_specs=[scalars, scalars, left, left] + [whole] * 12,
        out_specs=(left,) * (layers + 3),
        scratch_shapes=[
            vm(own, width, toks, f32),
            vm(layers, own, width, toks, f32),
            vm(layers, own, 1, toks, f32),
            vm(layers, own, width + ones_rows, toks, bf16),
            vm(layers, own, 3 * width, toks, bf16),
            vm(layers, own, toks, width, bf16),
            vm(layers, own, heads, toks, toks, bf16),
            vm(layers, own, heads, 1, toks, f32),
            vm(layers, own, width + ones_rows, toks, bf16),
            vm(layers, own, width, toks, f32),
            vm(layers, own, 1, toks, f32),
            vm(layers, own, width + ones_rows, toks, bf16),
            vm(layers, own, units + ones_rows, toks, bf16),
            vm(layers, own, units, toks, bf16),
            vm(layers, 3 * width, width, bf16),
            vm(layers, width, 3 * width, bf16),
            vm(layers, width, width, bf16),
            vm(layers, units, width, bf16),
            vm(layers, width, units, bf16),
            vm(layers, 9 * width + units, lane, f32),
            vm(toks // 2, toks // 2, f32),
            vm(layers, 3 * width, width + ones_rows, f32),
            vm(layers, width + ones_rows, width, f32),
            vm(layers, width + ones_rows, units, f32),
            vm(layers, units + ones_rows, width, f32),
            vm(layers, 4 * width, toks, f32),
            vm(own, toks, width, bf16),
            vm(own, heads, toks, toks, bf16),
            vm(own, width, toks, bf16),
            vm(own, units, toks, bf16),
            vm(own, width, toks, bf16),
            vm(own, 3 * width, toks, bf16),
            vm(heads, sizes.vec, width, f32),
            vm(heads, own, hd, toks, bf16),
            vm(heads, own, hd, toks, bf16),
            vm(8, lane, f32),
            vm(heads, 8, lane, f32),
            dma((heads - 1,)),
            dma((heads - 1,)),
            dma((heads - 1,)),
            dma((heads - 1,)),
            dma((heads - 1,)),
            dma((heads - 1,)),
            dma((heads - 1, own)),
            dma((heads - 1, own)),
            dma((4,)),
            vm(win, sizes.block, width, bf16),
            vm(toks * own, width, f32),
            vm(own, width, toks, bf16),
            dma((2,)),
        ]
        + [
            ref
            for used, cuts, rows in sizes.early
            for ref in Reduction.scratch(sizes, rows, used, width, len(cuts) + 1)
        ]
        + Reduction.scratch(sizes, sizes.late, sizes.late_used, width, 1),
        compiler_params=pltpu.CompilerParams(
            vmem_limit_bytes=63 * 1024 * 1024, collective_id=0, has_side_effects=True
        ),
    )(count, sample, x, cot, shard, qv, *big, *small)


def finish_pass(sizes, lo, ig, *packets):
    layers, width, hd, share = sizes.layers, sizes.width, sizes.hd, sizes.share
    whole = pl.BlockSpec(memory_space=pltpu.VMEM)
    out = lambda *shape: jax.ShapeDtypeStruct(shape, f32)
    row = out(layers, width)
    final = (sizes.slots, hd, sizes.win)
    return pl.pallas_call(
        functools.partial(finish_body, sizes),
        out_shape=(
            jax.ShapeDtypeStruct(final, bf16),
            out(*final),
            row,
            row,
            out(layers, 3 * hd, width),
            out(layers, 2 * hd),
            out(layers, hd, width),
            row,
            row,
            row,
            out(layers, width, share),
            out(layers, share),
            out(layers, share, width),
            row,
        ),
        in_specs=[whole] * (2 + len(packets)),
        out_specs=(whole,) * 14,
        compiler_params=pltpu.CompilerParams(vmem_limit_bytes=60 * 1024 * 1024),
    )(lo, ig, *packets)


def shards(
    layer_input,
    cotangent,
    window_count,
    sample_weight,
    ln1_gain,
    ln1_shift,
    qkv_weight,
    qv_bias,
    out_weight,
    out_bias,
    ln2_gain,
    ln2_shift,
    up_weight,
    up_bias,
    down_weight,
    down_bias,
):
    slots, win, width = layer_input.shape
    layers, _, units = up_weight.shape
    sizes = Sizes(
        slots, win, width, layers, units, lax.axis_size("head"), lax.axis_size("dp")
    )
    lo, ig, *packets = exchange_pass(
        sizes,
        window_count,
        sample_weight,
        jnp.swapaxes(layer_input, 0, 1),
        jnp.swapaxes(cotangent, 0, 1),
        jnp.swapaxes(qkv_weight, 1, 2),
        qv_bias,
        (out_weight, up_weight, down_weight),
        (ln1_gain, ln1_shift, out_bias, ln2_gain, ln2_shift, down_bias, up_bias),
    )
    outs = list(finish_pass(sizes, lo, ig, *packets))
    for index in (0, 1, 4):
        outs[index] = jnp.swapaxes(outs[index], 1, 2)
    return tuple(outs)


def solution(mesh):
    return jax.shard_map(
        shards,
        mesh=mesh,
        in_specs=(
            P("dp", None, None),
            P("dp", None, None),
            P("dp"),
            P("dp"),
            P(),
            P(),
            P(None, None, "head"),
            P(None, "head"),
            P(),
            P(),
            P(),
            P(),
            P(),
            P(),
            P(),
            P(),
        ),
        out_specs=(
            P("dp", None, "head"),
            P("dp", None, "head"),
            P(),
            P(),
            P(None, None, "head"),
            P(None, "head"),
            P(None, "head", None),
            P(),
            P(),
            P(),
            P(None, None, "head"),
            P(None, "head"),
            P(None, "head", None),
            P(),
        ),
        check_vma=False,
    )
```

```python
import functools
import math

import jax
import jax.numpy as jnp
from jax import lax
from jax.experimental import pallas as pl
from jax.experimental.pallas import tpu as pltpu
from jax.sharding import PartitionSpec as P

norm_eps = 1e-05
lane = 128
ones_rows = 16
group_size = 8
log2_e = 1.4426950408889634
far_below = -1e30
bf16 = jnp.bfloat16
f32 = jnp.float32


def nn(left, right):
    return lax.dot_general(left, right, (((1,), (0,)), ((), ())), preferred_element_type=f32)


def nt(left, right):
    return lax.dot_general(left, right, (((1,), (1,)), ((), ())), preferred_element_type=f32)


def nt_split(left, right):
    high = right.astype(bf16)
    return nt(left, high) + nt(left, (right - high.astype(f32)).astype(bf16))


def wide(column, width):
    return jnp.concatenate([column] * (width // lane), axis=1)


def gelu_parts(pre):
    cdf = 0.5 * lax.erf(pre * math.sqrt(0.5)) + 0.5
    bell = jnp.exp2((pre * pre) * (-0.5 * log2_e) + math.log2(1.0 / math.sqrt(2.0 * math.pi)))
    return pre * cdf, cdf + pre * bell


def eye(size):
    rows = lax.broadcasted_iota(jnp.int32, (size, size), 0)
    cols = lax.broadcasted_iota(jnp.int32, (size, size), 1)
    return (rows == cols).astype(f32).astype(bf16)


def side_by_side(works, between={}):
    works = [work for work in works if work is not None]
    turn = 0
    while works:
        if turn in between:
            between[turn]()
        works = [work for work in works if next(work, work) is None]
        turn += 1


def fold(block, act):
    rows = [block[i : i + 8] for i in range(0, block.shape[0], 8)]
    return functools.reduce(act, rows)


def spread_rows(block, h, heads):
    size, toks = block.shape
    parts = []
    if h:
        parts.append(jnp.zeros((h * size, toks), block.dtype))
    parts.append(block)
    if h < heads - 1:
        parts.append(jnp.zeros(((heads - 1 - h) * size, toks), block.dtype))
    return jnp.concatenate(parts, axis=0)


class Sizes:
    def __init__(self, slots, win, width, layers, units, heads, groups):
        self.slots, self.win, self.width = slots, win, width
        self.layers, self.units, self.heads, self.groups = layers, units, heads, groups
        self.hd = width // heads
        self.share = units // heads
        self.toks = -(-win // lane) * lane
        self.own = slots // heads
        self.block = 16 if self.own < 16 else self.own
        self.upper_rows = 3 * self.hd + self.hd + width + self.share
        self.first_rows = self.hd + width + self.share
        step = 16 * groups
        round_up = lambda rows: -(-rows // step) * step
        self.early = [
            (self.first_rows, (), round_up(self.first_rows))
            if l == 0
            else (self.upper_rows, (self.first_rows,), round_up(self.upper_rows))
            for l in range(layers)
        ]
        self.late_vec = 3 * self.hd
        self.vec = 16 * -(-8 * layers // 16)
        self.late_used = self.late_vec + self.vec
        self.late = round_up(self.late_used)

    def key(self):
        return (self.slots, self.win, self.width, self.layers, self.units, self.heads, self.groups)


class Reduction:
    def __init__(self, sizes, rows, used, cuts, done, refs):
        self.sizes, self.rows, self.used = sizes, rows, used
        self.chunk = rows // sizes.groups
        (
            self.out_buf,
            self.head_in,
            self.mid,
            self.dp_in,
            self.total,
            self.head_send,
            self.head_recv,
            self.dp_send,
            self.dp_recv,
            self.all_send,
            self.all_recv,
            self.own_sem,
        ) = refs
        self.done = done
        self.cuts = [0] + list(cuts) + [used]
        self.me = lax.axis_index("head")
        self.group = lax.axis_index("dp")

    @staticmethod
    def scratch(sizes, rows, used, width, parts):
        chunk = rows // sizes.groups
        vm = pltpu.VMEM
        dma = pltpu.SemaphoreType.DMA
        return [
            vm((sizes.heads, used, width), bf16),
            vm((sizes.heads - 1, used, width), bf16),
            vm((rows, width), bf16),
            vm((sizes.groups - 1, chunk, width), bf16),
            vm((chunk, width), bf16),
            dma((parts, sizes.heads - 1)),
            dma((parts, sizes.heads - 1)),
            dma((sizes.groups - 1,)),
            dma((sizes.groups - 1,)),
            dma((sizes.groups - 1,)),
            dma((sizes.groups - 1,)),
            dma((1,)),
        ]

    def head_copy(self, k, i):
        peer = lax.rem(self.me + k, self.sizes.heads)
        span = pl.ds(self.cuts[i], self.cuts[i + 1] - self.cuts[i])
        return pltpu.make_async_remote_copy(
            src_ref=self.out_buf.at[peer, span],
            dst_ref=self.head_in.at[k - 1, span],
            send_sem=self.head_send.at[i, k - 1],
            recv_sem=self.head_recv.at[i, k - 1],
            device_id={"head": peer},
            device_id_type=pl.DeviceIdType.MESH,
        )

    def part(self, index):
        return pl.ds(pl.multiple_of(index * self.chunk, 16), self.chunk)

    def dp_copy(self, k):
        peer = lax.rem(self.group + k, self.sizes.groups)
        return pltpu.make_async_remote_copy(
            src_ref=self.mid.at[self.part(peer)],
            dst_ref=self.dp_in.at[k - 1],
            send_sem=self.dp_send.at[k - 1],
            recv_sem=self.dp_recv.at[k - 1],
            device_id={"dp": peer},
            device_id_type=pl.DeviceIdType.MESH,
        )

    def all_copy(self, k):
        peer = lax.rem(self.group + k, self.sizes.groups)
        return pltpu.make_async_remote_copy(
            src_ref=self.total,
            dst_ref=self.done.at[self.part(self.group)],
            send_sem=self.all_send.at[k - 1],
            recv_sem=self.all_recv.at[k - 1],
            device_id={"dp": peer},
            device_id_type=pl.DeviceIdType.MESH,
        )

    def start_heads(self, i):
        for k in range(1, self.sizes.heads):
            self.head_copy(k, i).start()

    def start_groups(self):
        for i in range(len(self.cuts) - 1):
            for k in range(1, self.sizes.heads):
                self.head_copy(k, i).wait()
        total = self.out_buf[self.me].astype(f32)
        for k in range(1, self.sizes.heads):
            total += self.head_in[k - 1].astype(f32)
        self.mid[: self.used] = total.astype(bf16)
        each_peer(self.sizes.groups, lambda k: self.dp_copy(k).start())

    def start_gather(self):
        each_peer(self.sizes.groups, lambda k: self.dp_copy(k).wait())
        own = self.part(self.group)
        total = self.mid[own].astype(f32)
        for k in range(1, self.sizes.groups):
            total += self.dp_in[k - 1].astype(f32)
        self.total[...] = total.astype(bf16)
        self.own_copy().start()
        each_peer(self.sizes.groups, lambda k: self.all_copy(k).start())

    def own_copy(self):
        return pltpu.make_async_copy(
            self.total, self.done.at[self.part(self.group)], self.own_sem.at[0]
        )

    def finish(self):
        self.own_copy().wait()
        each_peer(self.sizes.groups, lambda k: self.all_copy(k).wait())


def each_peer(count, act):
    def step(k, carry):
        act(k)
        return carry

    if count <= 8:
        for k in range(1, count):
            act(k)
    else:
        lax.fori_loop(1, count, step, 0)


def body(sizes, *refs):
    inputs = 18
    early_refs = refs[inputs : inputs + sizes.layers]
    exchange(sizes, early_refs, *refs[:inputs], *refs[inputs + sizes.layers :])


def exchange(
    sizes,
    early_refs,
    count_ref,
    sample_ref,
    x_ref,
    cot_ref,
    qkv_shard_ref,
    qv_ref,
    out_w_ref,
    up_w_ref,
    down_w_ref,
    g1_ref,
    b1_ref,
    bo_ref,
    g2_ref,
    b2_ref,
    bd_ref,
    bu_ref,
    lo_ref,
    ig_ref,
    late_ref,
    stream,
    xh1,
    rs1,
    n1e,
    qkv,
    v_tok,
    probs,
    inv,
    att,
    xh2,
    rs2,
    n2e,
    act,
    slope,
    qkv_t_ref,
    qkv_n,
    out_t,
    up_t,
    down_t,
    cols,
    mask,
    g_qkv,
    g_out,
    g_up,
    g_down,
    g_vec,
    k_tok,
    g_scr,
    gl_kept,
    gp_kept,
    gm_kept,
    gqkv_kept,
    vec_rows,
    lo_stage,
    ig_stage,
    qv_own,
    qv_all,
    shard_send,
    shard_recv,
    qv_send,
    qv_recv,
    lo_send,
    lo_recv,
    ig_send,
    ig_recv,
    own_sem,
    x_in,
    x_rows,
    cot_t,
    in_sem,
    *reduction_refs,
):
    layers, heads, width, units = sizes.layers, sizes.heads, sizes.width, sizes.units
    win, toks, own, hd, share = sizes.win, sizes.toks, sizes.own, sizes.hd, sizes.share
    scale = 1.0 / math.sqrt(hd)
    half = toks // 2
    abreast = math.gcd(own, group_size)
    me = lax.axis_index("head")
    group = lax.axis_index("dp")
    earlies = [
        Reduction(sizes, rows, used, cuts, early_refs[l], reduction_refs[12 * l : 12 * (l + 1)])
        for l, (used, cuts, rows) in enumerate(sizes.early)
    ]
    late = Reduction(sizes, sizes.late, sizes.late_used, (sizes.late_vec,), late_ref, reduction_refs[12 * layers :])

    def head_peer(k):
        return lax.rem(me + k, heads)

    first = me * own
    fetch_from = pl.multiple_of(first // sizes.block * sizes.block, 16)
    fetches = [
        pltpu.make_async_copy(src.at[:, pl.ds(fetch_from, sizes.block)], dst, in_sem.at[i])
        for i, (src, dst) in enumerate(((x_ref, x_in), (cot_ref, x_in)))
    ]
    fetches[0].start()
    barrier = pltpu.get_barrier_semaphore()
    for k in range(1, heads):
        pl.semaphore_signal(
            barrier, inc=1, device_id={"head": head_peer(k)}, device_id_type=pl.DeviceIdType.MESH
        )

    def greet(k):
        pl.semaphore_signal(
            barrier,
            inc=1,
            device_id={"dp": lax.rem(group + k, sizes.groups)},
            device_id_type=pl.DeviceIdType.MESH,
        )

    each_peer(sizes.groups, greet)

    c_g1, c_b1, c_qkv, c_bo = 0, width, 2 * width, 5 * width
    c_g2, c_b2, c_bd, c_up = 6 * width, 7 * width, 8 * width, 9 * width

    identity = eye(width)
    identity_tok = eye(toks)

    def row_to_column(row):
        return jnp.transpose(jnp.broadcast_to(row, (lane, lane)))

    qv_own[...] = jnp.zeros_like(qv_own)
    for l in range(layers):
        qv_own[l : l + 1, :hd] = qv_ref[l : l + 1, :hd]
        qv_own[l : l + 1, 2 * hd : 3 * hd] = qv_ref[l : l + 1, hd : 2 * hd]
    mine = pl.ds(pl.multiple_of(me * 3 * hd, 16), 3 * hd)
    own_shard = pltpu.make_async_copy(qkv_shard_ref, qkv_t_ref.at[:, mine], own_sem.at[0])
    own_qv = pltpu.make_async_copy(qv_own, qv_all.at[me], own_sem.at[1])

    def shard_copy(k):
        return pltpu.make_async_remote_copy(
            src_ref=qkv_shard_ref,
            dst_ref=qkv_t_ref.at[:, mine],
            send_sem=shard_send.at[k - 1],
            recv_sem=shard_recv.at[k - 1],
            device_id={"head": head_peer(k)},
            device_id_type=pl.DeviceIdType.MESH,
        )

    def qv_copy(k):
        return pltpu.make_async_remote_copy(
            src_ref=qv_own,
            dst_ref=qv_all.at[me],
            send_sem=qv_send.at[k - 1],
            recv_sem=qv_recv.at[k - 1],
            device_id={"head": head_peer(k)},
            device_id_type=pl.DeviceIdType.MESH,
        )

    pl.semaphore_wait(barrier, heads - 1 + sizes.groups - 1)
    own_shard.start()
    own_qv.start()
    for k in range(1, heads):
        qv_copy(k).start()
        shard_copy(k).start()

    def sort_rows(src, dst):
        step = 10 if win % 10 == 0 else 1
        for t in range(0, win, step):
            block = src[t : t + step].astype(f32)
            rows = block[:, :own]
            for i in range(1, sizes.block // own):
                here = first - fetch_from == i * own
                rows = jnp.where(here, block[:, i * own : (i + 1) * own], rows)
            dst[t * own : (t + step) * own] = rows.reshape(step * own, width)
        dst[win * own :] = jnp.zeros(((toks - win) * own, width), f32)

    def turned(src, w):
        return nt(identity, src[pl.ds(w, toks, stride=own), :].astype(bf16))

    def put_column(l, start, ref):
        cols[l, start : start + width] = row_to_column(ref[l : l + 1, :])

    for l in range(layers):
        out_t[l] = nt(identity, out_w_ref[l]).astype(bf16)
        for part in range(units // width):
            span = slice(part * width, (part + 1) * width)
            up_t[l, span, :] = jnp.transpose(up_w_ref[l, :, span].astype(f32)).astype(bf16)
            cols[l, c_up + part * width : c_up + (part + 1) * width] = row_to_column(
                bu_ref[l : l + 1, span]
            )
        down_t[l] = nt(identity, down_w_ref[l]).astype(bf16)
        for start, ref in (
            (c_bo, bo_ref),
            (c_g2, g2_ref),
            (c_b2, b2_ref),
            (c_bd, bd_ref),
        ):
            put_column(l, start, ref)
        put_column(l, c_g1, g1_ref)
        put_column(l, c_b1, b1_ref)
    key_pos = lax.broadcasted_iota(jnp.int32, (half, half), 0)
    query_pos = lax.broadcasted_iota(jnp.int32, (half, half), 1)
    mask[...] = jnp.where(key_pos <= query_pos, 0.0, far_below)
    g_vec[...] = jnp.zeros_like(g_vec)
    vec_rows[...] = jnp.zeros_like(vec_rows)
    for packet in earlies + [late]:
        if packet.rows > packet.used:
            packet.mid[packet.used :] = jnp.zeros((packet.rows - packet.used, width), bf16)

    for w in range(own):
        for l in range(layers):
            n1e[l, w, width:, :] = jnp.ones((ones_rows, toks), bf16)
            n2e[l, w, width:, :] = jnp.ones((ones_rows, toks), bf16)
            att[l, w, width:, :] = jnp.ones((ones_rows, toks), bf16)
            act[l, w, units:, :] = jnp.ones((ones_rows, toks), bf16)
        for h in range(heads):
            g_scr[w, h, half:, :half] = jnp.zeros((half, half), bf16)
            for l in range(layers):
                probs[l, w, h, half:, :half] = jnp.zeros((half, half), bf16)

    fetches[0].wait()
    sort_rows(x_in, x_rows)
    fetches[1].start()
    for w in range(own):
        stream[w] = turned(x_rows, w)

    fetches[1].wait()
    sort_rows(x_in, x_rows)
    for w in range(own):
        cot_t[w] = turned(x_rows, w).astype(bf16)

    def col(l, start, count):
        return wide(cols[l, start : start + count, :], toks)

    step = hd


    def spans(start, count):
        return [slice(r, r + step) for r in range(start, start + count, step)]

    def norm(w, l, gain, shift, unit_ref, spread_ref, low_ref):
        total = sum(fold(stream[w, r], jnp.add) for r in spans(0, width))
        mean = jnp.sum(total, axis=0, keepdims=True) * (1.0 / width)
        square = 0.0
        for r in spans(0, width):
            center = stream[w, r] - mean
            square += fold(center * center, jnp.add)
        spread = lax.rsqrt(jnp.sum(square, axis=0, keepdims=True) * (1.0 / width) + norm_eps)
        spread_ref[l, w] = spread
        for r in spans(0, width):
            unit = (stream[w, r] - mean) * spread
            unit_ref[l, w, r] = unit
            low_ref[l, w, r] = (
                unit * col(l, gain + r.start, step) + col(l, shift + r.start, step)
            ).astype(bf16)

    for w in range(own):
        norm(w, 0, c_g1, c_b1, xh1, rs1, n1e)
    own_shard.wait()
    own_qv.wait()
    for k in range(1, heads):
        qv_copy(k).wait()
        shard_copy(k).wait()
    for l in range(layers):
        qkv_n[l] = nt(identity, qkv_t_ref[l]).astype(bf16)
        for h in range(heads):
            cols[l, c_qkv + 3 * hd * h : c_qkv + 3 * hd * (h + 1)] = row_to_column(
                qv_all[h, l : l + 1, :]
            )[: 3 * hd]
    def forward(l, w):
        if l:
            norm(w, l, c_g1, c_b1, xh1, rs1, n1e)
            yield
        made = nn(qkv_t_ref[l], n1e[l, w, :width])
        for i, r in enumerate(spans(0, 3 * width)):
            piece = made[r] + col(l, c_qkv + r.start, step)
            qkv[l, w, r] = (piece if i % 3 else piece * (scale * log2_e)).astype(bf16)
        yield
        rows_of = lambda h, which: slice((3 * h + which) * hd, (3 * h + which + 1) * hd)
        kv_all = jnp.concatenate(
            [qkv[l, w, rows_of(h, which)] for which in (1, 2) for h in range(heads)], axis=0
        )
        made = nt(identity_tok, kv_all)
        for r in spans(0, toks):
            k_tok[w, r] = made[r, :width].astype(bf16)
            v_tok[l, w, r] = made[r, width:].astype(bf16)
        for h in range(heads):
            yield
            s = nn(k_tok[w], spread_rows(qkv[l, w, rows_of(h, 0)], h, heads))
            top0 = top1 = None
            for r in spans(0, half):
                far = slice(r.start + half, r.stop + half)
                new0 = fold(s[r, :half] + mask[r], jnp.maximum)
                new1 = jnp.maximum(
                    fold(s[r, half:], jnp.maximum), fold(s[far, half:] + mask[r], jnp.maximum)
                )
                top0 = new0 if top0 is None else jnp.maximum(top0, new0)
                top1 = new1 if top1 is None else jnp.maximum(top1, new1)
            top0 = jnp.max(top0, axis=0, keepdims=True)
            top1 = jnp.max(top1, axis=0, keepdims=True)
            for r in spans(0, half):
                far = slice(r.start + half, r.stop + half)
                probs[l, w, h, r, :half] = jnp.exp2(s[r, :half] + mask[r] - top0).astype(bf16)
                probs[l, w, h, r, half:] = jnp.exp2(s[r, half:] - top1).astype(bf16)
                probs[l, w, h, far, half:] = jnp.exp2(s[far, half:] + mask[r] - top1).astype(bf16)
            yield
            v_ext = jnp.concatenate(
                [qkv[l, w, rows_of(h, 2)], jnp.ones((ones_rows, toks), bf16)], axis=0
            )
            o = nn(v_ext, probs[l, w, h])
            inverse = 1.0 / o[hd : hd + 1]
            inv[l, w, h] = inverse
            att[l, w, hd * h : hd * (h + 1)] = (o[:hd] * inverse).astype(bf16)
        yield
        made = nn(out_t[l], att[l, w, :width])
        for r in spans(0, width):
            stream[w, r] = stream[w, r] + made[r] + col(l, c_bo + r.start, step)
        norm(w, l, c_g2, c_b2, xh2, rs2, n2e)
        yield
        made = nn(up_t[l], n2e[l, w, :width])
        for r in spans(0, units):
            a, sl = gelu_parts(made[r] + col(l, c_up + r.start, step))
            act[l, w, r] = a.astype(bf16)
            slope[l, w, r] = sl.astype(bf16)
        yield
        made = nn(down_t[l], act[l, w, :units])
        for r in spans(0, width):
            value = stream[w, r] + made[r] + col(l, c_bd + r.start, step)
            if l < layers - 1:
                stream[w, r] = value
            else:
                lo_stage[r.start // hd, w] = value.astype(bf16)

    def norm_sums(l, w, grad, gain, unit_ref, which):
        plain = tilted = 0.0
        for r in spans(0, width):
            by_unit = grad[r] * unit_ref[l, w, r]
            at = slice(which * width + r.start, which * width + r.stop)
            g_vec[l, at] += by_unit
            at = slice((which + 1) * width + r.start, (which + 1) * width + r.stop)
            g_vec[l, at] += grad[r]
            column = col(l, gain + r.start, step)
            plain += fold(grad[r] * column, jnp.add)
            tilted += fold(by_unit * column, jnp.add)
        return (
            jnp.sum(plain, axis=0, keepdims=True) * (1.0 / width),
            jnp.sum(tilted, axis=0, keepdims=True) * (1.0 / width),
        )

    def norm_back(l, w, grad, gain, unit_ref, spread_ref, means, emit):
        spread = spread_ref[l, w]
        for r in spans(0, width):
            s = grad[r] * col(l, gain + r.start, step)
            emit(r, stream[w, r] + spread * (s - means[0] - unit_ref[l, w, r] * means[1]))

    def backward_units(l, w):
        if l == layers - 1:
            slot = me * own + w
            weight = jnp.where(slot < count_ref[0], sample_ref[slot], 0.0)
        for r in spans(0, width):
            if l == layers - 1:
                stream[w, r] = cot_t[w, r].astype(f32) * weight
            gl_kept[w, r] = stream[w, r].astype(bf16)
        yield
        made = nn(down_w_ref[l], gl_kept[w])
        for r in spans(0, units):
            gp_kept[w, r] = made[r].astype(bf16) * slope[l, w, r]
        yield
        gn = nn(up_w_ref[l], gp_kept[w])
        yield
        means = norm_sums(l, w, gn, c_g2, xh2, 2)

        def emit(r, value):
            stream[w, r] = value
            gm_kept[w, r] = value.astype(bf16)

        norm_back(l, w, gn, c_g2, xh2, rs2, means, emit)

    def backward_attention(l, w, after):
        ga = nn(out_w_ref[l], gm_kept[w])
        shares, dots = [], []
        for h in range(heads):
            rows = slice(h * hd, (h + 1) * hd)
            gs = (ga[rows] * inv[l, w, h]).astype(bf16)
            shares.append(gs)
            dots.append(
                jnp.sum(gs.astype(f32) * att[l, w, rows, :].astype(f32), axis=0, keepdims=True)
            )
        yield
        for h in range(heads):
            base = 3 * h * hd
            yield
            gs, dot = shares[h], dots[h]
            made = nn(v_tok[l, w], spread_rows(gs, h, heads))
            gqkv_kept[w, base + 2 * hd : base + 3 * hd] = nt(gs, probs[l, w, h]).astype(bf16)
            d0, d1 = dot[:, :half], dot[:, half:]
            for r in spans(0, half):
                far = slice(r.start + half, r.stop + half)
                g_scr[w, h, r, :half] = probs[l, w, h, r, :half] * (made[r, :half] - d0).astype(bf16)
                g_scr[w, h, r, half:] = probs[l, w, h, r, half:] * (made[r, half:] - d1).astype(bf16)
                g_scr[w, h, far, half:] = probs[l, w, h, far, half:] * (
                    made[far, half:] - d1
                ).astype(bf16)
            yield
            q = qkv[l, w, base : base + hd, :]
            k = qkv[l, w, base + hd : base + 2 * hd, :]
            g = g_scr[w, h]
            gq = (nn(k, g) * scale).astype(bf16)
            gk = (nt(q, g) * (1.0 / log2_e)).astype(bf16)
            gqkv_kept[w, base : base + hd] = gq
            gqkv_kept[w, base + hd : base + 2 * hd] = gk
        yield
        gn = nn(qkv_n[l], gqkv_kept[w])
        yield
        means = norm_sums(l, w, gn, c_g1, xh1, 0)
        after(w, gn, means)

    def lanes(ref, ws):
        return jnp.concatenate([ref[w] for w in ws], axis=1)

    def unit_sums(l, ws):
        def add(ref, value):
            ref[l] = value if ws[0] == 0 else ref[l] + value

        add(g_down, nt(lanes(act.at[l], ws), lanes(gl_kept, ws)))
        add(g_up, nt(lanes(n2e.at[l], ws), lanes(gp_kept, ws)))
        add(g_out, nt(lanes(att.at[l], ws), lanes(gm_kept, ws)))

    def qkv_sums(l, ws):
        value = nt(lanes(gqkv_kept, ws), lanes(n1e.at[l], ws))
        g_qkv[l] = value if ws[0] == 0 else g_qkv[l] + value

    def run(step, first, last, width=1):
        def inner(i, carry):
            side_by_side([step(first + i * width + u) for u in range(width)])
            return carry

        if last - first == width:
            inner(0, 0)
        else:
            lax.fori_loop(0, (last - first) // width, inner, 0)

    last = math.gcd(own, 4)
    cut = own - last

    def lo_copy(k):
        peer = head_peer(k)
        return pltpu.make_async_remote_copy(
            src_ref=lo_stage.at[peer],
            dst_ref=lo_ref.at[pl.ds(me * own, own)],
            send_sem=lo_send.at[k - 1],
            recv_sem=lo_recv.at[k - 1],
            device_id={"head": peer},
            device_id_type=pl.DeviceIdType.MESH,
        )

    def ig_copy(k, i):
        peer = head_peer(k)
        return pltpu.make_async_remote_copy(
            src_ref=ig_stage.at[peer, pl.ds(i * last, last)],
            dst_ref=ig_ref.at[pl.ds(me * own + i * last, last)],
            send_sem=ig_send.at[k - 1, i],
            recv_sem=ig_recv.at[k - 1, i],
            device_id={"head": peer},
            device_id_type=pl.DeviceIdType.MESH,
        )

    for l in range(layers):
        run(functools.partial(forward, l), 0, own, abreast)

    own_lo = pltpu.make_async_copy(
        lo_stage.at[me], lo_ref.at[pl.ds(me * own, own)], own_sem.at[2]
    )
    own_lo.start()
    for k in range(1, heads):
        lo_copy(k).start()

    def vector_rows(l, norm_index):
        at = slice(2 * norm_index * width, 2 * (norm_index + 1) * width)
        return nt_split(jnp.ones((16, toks), bf16), g_vec[l, at])

    def qkv_bias_rows(l):
        at = lax.broadcasted_iota(jnp.int32, (16, width + ones_rows), 1)
        return nt_split((at == width).astype(f32).astype(bf16), g_qkv[l])

    def pack_units(l):
        buf = earlies[l].out_buf
        for h in range(heads):
            at = 0
            buf[h, at : at + hd] = g_out[l, hd * h : hd * (h + 1), :].astype(bf16)
            at += hd
            buf[h, at : at + width] = g_up[l, :width, share * h : share * (h + 1)].astype(bf16)
            at += width
            buf[h, at : at + share] = g_down[l, share * h : share * (h + 1), :].astype(bf16)

    def pack_qkv(l):
        r = sizes.first_rows
        for h in range(heads):
            earlies[l].out_buf[h, r : r + 3 * hd] = g_qkv[
                l, 3 * hd * h : 3 * hd * (h + 1), :width
            ].astype(bf16)

    def put_row(at, row):
        for h in range(heads):
            vec_rows[h, at : at + 1] = row

    def put_norm(l, norm_index, at):
        sums = vector_rows(l, norm_index)
        put_row(at, sums[:1, :width])
        put_row(at + 1, sums[:1, width:])

    def put_qkv(l):
        biases = qkv_bias_rows(l)
        for h in range(heads):
            for i in range(3):
                at = (3 * h + i) * hd
                vec_rows[h, 8 * l + 7 : 8 * l + 8, i * hd : (i + 1) * hd] = biases[:1, at : at + hd]

    def pack_vectors():
        for l in range(layers):
            v = 8 * l
            if l:
                put_norm(l, 0, v)
                put_qkv(l)
            put_row(v + 2, g_out[l, width : width + 1, :])
            put_norm(l, 1, v + 3)
            put_row(v + 5, g_down[l, units : units + 1, :])
            for h in range(heads):
                vec_rows[h, v + 6 : v + 7] = g_up[
                    l, width : width + 1, share * h : share * (h + 1)
                ]

    def pack_late_weights():
        for h in range(heads):
            late.out_buf[h, : 3 * hd] = g_qkv[0, 3 * hd * h : 3 * hd * (h + 1), :width].astype(
                bf16
            )

    def pack_late_vectors():
        ones = jnp.ones((16, toks * own), bf16)
        for h in range(heads):
            rows = slice(3 * hd * h, 3 * hd * (h + 1))
            grads = jnp.concatenate([gqkv_kept[w, rows] for w in everyone], axis=1)
            vec_rows[h, 7:8, : 3 * hd] = nt(ones, grads)[:1]
        put_norm(0, 0, 0)
        for h in range(heads):
            late.out_buf[h, 3 * hd :] = vec_rows[h].astype(bf16)

    def give(w, gn, means):
        def emit(r, value):
            ig_stage[r.start // hd, w] = value.astype(bf16)

        norm_back(0, w, gn, c_g1, xh1, rs1, means, emit)
    waiting = {}

    def keep(w, gn, means):
        for i in range(toks // lane):
            at = (w * (toks // lane) + i) * width
            x_rows[at : at + width] = gn[:, i * lane : (i + 1) * lane]
        waiting[w] = means

    everyone = list(range(own))
    for l in range(layers - 1, -1, -1):
        run(functools.partial(backward_units, l), 0, own, abreast)
        steps = {}
        if l < layers - 1:
            steps[heads + 2] = earlies[l + 1].start_gather
        if l:

            def settle(w, gn, means, l=l):
                def emit(r, value):
                    stream[w, r] = value

                norm_back(l, w, gn, c_g1, xh1, rs1, means, emit)

            def unit_step(l=l):
                unit_sums(l, everyone)
                pack_units(l)
                earlies[l].start_heads(0)

            steps[heads] = unit_step
        else:
            settle = keep
            unit_sums(l, everyone)
            pack_units(l)
            earlies[l].start_heads(0)
            steps[2] = pack_vectors
            steps[2 * heads] = earlies[l].start_groups
        if l < layers - 1:
            earlies[l + 1].start_groups()
        side_by_side([backward_attention(l, w, after=settle) for w in everyone], steps)
        if l:
            qkv_sums(l, everyone)
            pack_qkv(l)
            earlies[l].start_heads(1)

    qkv_sums(0, everyone)
    pack_late_weights()
    late.start_heads(0)
    pack_late_vectors()
    late.start_heads(1)
    earlies[0].start_gather()
    batches = own // last

    def give_batch(i):
        for w in everyone[i * last : (i + 1) * last]:
            at = w * (toks // lane) * width
            halves = [x_rows[at + i * width : at + (i + 1) * width] for i in range(toks // lane)]
            give(w, jnp.concatenate(halves, axis=1), waiting[w])

    def send_batch(i):
        for k in range(1, heads):
            ig_copy(k, i).start()

    for i in range(batches - 1):
        give_batch(i)
        send_batch(i)
    give_batch(batches - 1)
    own_ig = pltpu.make_async_copy(
        ig_stage.at[me], ig_ref.at[pl.ds(me * own, own)], own_sem.at[3]
    )
    late.start_groups()
    send_batch(batches - 1)
    own_ig.start()
    own_lo.wait()
    for k in range(1, heads):
        lo_copy(k).wait()
    late.start_gather()
    for packet in earlies:
        packet.finish()
    for i in range(batches):
        for k in range(1, heads):
            ig_copy(k, i).wait()
    own_ig.wait()
    late.finish()


def finish_body(sizes, lo_in, ig_in, *refs):
    packets = refs[: sizes.layers + 1]
    write_outputs(sizes, lo_in, ig_in, packets[:-1], packets[-1], *refs[sizes.layers + 1 :])


def write_outputs(
    sizes,
    lo_in,
    ig_in,
    earlies_in,
    late_in,
    lo_out,
    ig_out,
    ln1_g,
    ln1_s,
    qkv_g,
    qv_g,
    out_g,
    out_b,
    ln2_g,
    ln2_s,
    up_g,
    up_b,
    down_g,
    down_b,
):
    hd, width, share = sizes.hd, sizes.width, sizes.share
    lo_out[...] = lo_in[...][:, :, : sizes.win]
    ig_out[...] = ig_in[...][:, :, : sizes.win].astype(f32)
    for l in range(sizes.layers):
        at = 0
        early_in = earlies_in[l]
        out_g[l] = early_in[at : at + hd].astype(f32)
        at += hd
        up_g[l] = early_in[at : at + width].astype(f32)
        at += width
        down_g[l] = early_in[at : at + share].astype(f32)
        at += share
        if l:
            qkv_g[l] = early_in[at : at + 3 * hd].astype(f32)
            at += 3 * hd
        else:
            qkv_g[l] = late_in[: 3 * hd].astype(f32)
    vec = late_in[3 * hd : 3 * hd + sizes.vec].astype(f32)
    for l in range(sizes.layers):
        v = 8 * l
        row = slice(l, l + 1)
        ln1_g[row] = vec[v : v + 1]
        ln1_s[row] = vec[v + 1 : v + 2]
        out_b[row] = vec[v + 2 : v + 3]
        ln2_g[row] = vec[v + 3 : v + 4]
        ln2_s[row] = vec[v + 4 : v + 5]
        down_b[row] = vec[v + 5 : v + 6]
        up_b[row] = vec[v + 6 : v + 7]
        qv = vec[v + 7 : v + 8]
        qv_g[row, :hd] = qv[:, :hd]
        qv_g[row, hd:] = qv[:, 2 * hd : 3 * hd]


def exchange_pass(sizes, count, sample, x, cot, shard, qv, big, small):
    layers, heads, width, units = sizes.layers, sizes.heads, sizes.width, sizes.units
    own, toks, hd, win = sizes.own, sizes.toks, sizes.hd, sizes.win
    vm = lambda *shape: pltpu.VMEM(shape[:-1], shape[-1])
    dma = pltpu.SemaphoreType.DMA
    whole = pl.BlockSpec(memory_space=pltpu.VMEM)
    scalars = pl.BlockSpec(memory_space=pltpu.SMEM)
    left = pl.BlockSpec(memory_space=pl.ANY)
    return pl.pallas_call(
        functools.partial(body, sizes),
        out_shape=(
            jax.ShapeDtypeStruct((sizes.slots, hd, toks), bf16),
            jax.ShapeDtypeStruct((sizes.slots, hd, toks), bf16),
            *[jax.ShapeDtypeStruct((rows, width), bf16) for _, _, rows in sizes.early],
            jax.ShapeDtypeStruct((sizes.late, width), bf16),
        ),
        in_specs=[scalars, scalars, left, left] + [whole] * 12,
        out_specs=(left,) * (layers + 3),
        scratch_shapes=[
            vm(own, width, toks, f32),
            vm(layers, own, width, toks, f32),
            vm(layers, own, 1, toks, f32),
            vm(layers, own, width + ones_rows, toks, bf16),
            vm(layers, own, 3 * width, toks, bf16),
            vm(layers, own, toks, width, bf16),
            vm(layers, own, heads, toks, toks, bf16),
            vm(layers, own, heads, 1, toks, f32),
            vm(layers, own, width + ones_rows, toks, bf16),
            vm(layers, own, width, toks, f32),
            vm(layers, own, 1, toks, f32),
            vm(layers, own, width + ones_rows, toks, bf16),
            vm(layers, own, units + ones_rows, toks, bf16),
            vm(layers, own, units, toks, bf16),
            vm(layers, 3 * width, width, bf16),
            vm(layers, width, 3 * width, bf16),
            vm(layers, width, width, bf16),
            vm(layers, units, width, bf16),
            vm(layers, width, units, bf16),
            vm(layers, 9 * width + units, lane, f32),
            vm(toks // 2, toks // 2, f32),
            vm(layers, 3 * width, width + ones_rows, f32),
            vm(layers, width + ones_rows, width, f32),
            vm(layers, width + ones_rows, units, f32),
            vm(layers, units + ones_rows, width, f32),
            vm(layers, 4 * width, toks, f32),
            vm(own, toks, width, bf16),
            vm(own, heads, toks, toks, bf16),
            vm(own, width, toks, bf16),
            vm(own, units, toks, bf16),
            vm(own, width, toks, bf16),
            vm(own, 3 * width, toks, bf16),
            vm(heads, sizes.vec, width, f32),
            vm(heads, own, hd, toks, bf16),
            vm(heads, own, hd, toks, bf16),
            vm(8, lane, f32),
            vm(heads, 8, lane, f32),
            dma((heads - 1,)),
            dma((heads - 1,)),
            dma((heads - 1,)),
            dma((heads - 1,)),
            dma((heads - 1,)),
            dma((heads - 1,)),
            dma((heads - 1, own)),
            dma((heads - 1, own)),
            dma((4,)),
            vm(win, sizes.block, width, bf16),
            vm(toks * own, width, f32),
            vm(own, width, toks, bf16),
            dma((2,)),
        ]
        + [
            ref
            for used, cuts, rows in sizes.early
            for ref in Reduction.scratch(sizes, rows, used, width, len(cuts) + 1)
        ]
        + Reduction.scratch(sizes, sizes.late, sizes.late_used, width, 2),
        compiler_params=pltpu.CompilerParams(
            vmem_limit_bytes=63 * 1024 * 1024, collective_id=0, has_side_effects=True
        ),
    )(count, sample, x, cot, shard, qv, *big, *small)


def finish_pass(sizes, lo, ig, *packets):
    layers, width, hd, share = sizes.layers, sizes.width, sizes.hd, sizes.share
    whole = pl.BlockSpec(memory_space=pltpu.VMEM)
    out = lambda *shape: jax.ShapeDtypeStruct(shape, f32)
    row = out(layers, width)
    final = (sizes.slots, hd, sizes.win)
    return pl.pallas_call(
        functools.partial(finish_body, sizes),
        out_shape=(
            jax.ShapeDtypeStruct(final, bf16),
            out(*final),
            row,
            row,
            out(layers, 3 * hd, width),
            out(layers, 2 * hd),
            out(layers, hd, width),
            row,
            row,
            row,
            out(layers, width, share),
            out(layers, share),
            out(layers, share, width),
            row,
        ),
        in_specs=[whole] * (2 + len(packets)),
        out_specs=(whole,) * 14,
        compiler_params=pltpu.CompilerParams(vmem_limit_bytes=60 * 1024 * 1024),
    )(lo, ig, *packets)


def shards(
    layer_input,
    cotangent,
    window_count,
    sample_weight,
    ln1_gain,
    ln1_shift,
    qkv_weight,
    qv_bias,
    out_weight,
    out_bias,
    ln2_gain,
    ln2_shift,
    up_weight,
    up_bias,
    down_weight,
    down_bias,
):
    slots, win, width = layer_input.shape
    layers, _, units = up_weight.shape
    sizes = Sizes(
        slots, win, width, layers, units, lax.axis_size("head"), lax.axis_size("dp")
    )
    lo, ig, *packets = exchange_pass(
        sizes,
        window_count,
        sample_weight,
        jnp.swapaxes(layer_input, 0, 1),
        jnp.swapaxes(cotangent, 0, 1),
        jnp.swapaxes(qkv_weight, 1, 2),
        qv_bias,
        (out_weight, up_weight, down_weight),
        (ln1_gain, ln1_shift, out_bias, ln2_gain, ln2_shift, down_bias, up_bias),
    )
    outs = list(finish_pass(sizes, lo, ig, *packets))
    for index in (0, 1, 4):
        outs[index] = jnp.swapaxes(outs[index], 1, 2)
    return tuple(outs)


def solution(mesh):
    return jax.shard_map(
        shards,
        mesh=mesh,
        in_specs=(
            P("dp", None, None),
            P("dp", None, None),
            P("dp"),
            P("dp"),
            P(),
            P(),
            P(None, None, "head"),
            P(None, "head"),
            P(),
            P(),
            P(),
            P(),
            P(),
            P(),
            P(),
            P(),
        ),
        out_specs=(
            P("dp", None, "head"),
            P("dp", None, "head"),
            P(),
            P(),
            P(None, None, "head"),
            P(None, "head"),
            P(None, "head", None),
            P(),
            P(),
            P(),
            P(None, None, "head"),
            P(None, "head"),
            P(None, "head", None),
            P(),
        ),
        check_vma=False,
    )
```

```python
import functools
import math

import jax
import jax.numpy as jnp
from jax import lax
from jax.experimental import pallas as pl
from jax.experimental.pallas import tpu as pltpu
from jax.sharding import PartitionSpec as P

norm_eps = 1e-05
lane = 128
ones_rows = 16
group_size = 8
log2_e = 1.4426950408889634
far_below = -1e30
bf16 = jnp.bfloat16
f32 = jnp.float32


def nn(left, right):
    return lax.dot_general(left, right, (((1,), (0,)), ((), ())), preferred_element_type=f32)


def nt(left, right):
    return lax.dot_general(left, right, (((1,), (1,)), ((), ())), preferred_element_type=f32)


def nt_split(left, right):
    high = right.astype(bf16)
    return nt(left, high) + nt(left, (right - high.astype(f32)).astype(bf16))


def wide(column, width):
    return jnp.concatenate([column] * (width // lane), axis=1)


def gelu_parts(pre):
    cdf = 0.5 * lax.erf(pre * math.sqrt(0.5)) + 0.5
    bell = jnp.exp2((pre * pre) * (-0.5 * log2_e) + math.log2(1.0 / math.sqrt(2.0 * math.pi)))
    return pre * cdf, cdf + pre * bell


def eye(size):
    rows = lax.broadcasted_iota(jnp.int32, (size, size), 0)
    cols = lax.broadcasted_iota(jnp.int32, (size, size), 1)
    return (rows == cols).astype(f32).astype(bf16)


def side_by_side(works, between={}):
    works = [work for work in works if work is not None]
    turn = 0
    while works:
        if turn in between:
            between[turn]()
        works = [work for work in works if next(work, work) is None]
        turn += 1


def fold(block, act):
    rows = [block[i : i + 8] for i in range(0, block.shape[0], 8)]
    return functools.reduce(act, rows)


def spread_rows(block, h, heads):
    size, toks = block.shape
    parts = []
    if h:
        parts.append(jnp.zeros((h * size, toks), block.dtype))
    parts.append(block)
    if h < heads - 1:
        parts.append(jnp.zeros(((heads - 1 - h) * size, toks), block.dtype))
    return jnp.concatenate(parts, axis=0)


class Sizes:
    def __init__(self, slots, win, width, layers, units, heads, groups):
        self.slots, self.win, self.width = slots, win, width
        self.layers, self.units, self.heads, self.groups = layers, units, heads, groups
        self.hd = width // heads
        self.share = units // heads
        self.toks = -(-win // lane) * lane
        self.own = slots // heads
        self.block = 16 if self.own < 16 else self.own
        self.upper_rows = 3 * self.hd + self.hd + width + self.share
        self.first_rows = self.hd + width + self.share
        step = 16 * groups
        round_up = lambda rows: -(-rows // step) * step
        self.early = [
            (self.first_rows, (), round_up(self.first_rows))
            if l == 0
            else (self.upper_rows, (self.first_rows,), round_up(self.upper_rows))
            for l in range(layers)
        ]
        self.late_vec = 3 * self.hd
        self.vec = 16 * -(-8 * layers // 16)
        self.late_used = self.late_vec + self.vec
        self.late = round_up(self.late_used)

    def key(self):
        return (self.slots, self.win, self.width, self.layers, self.units, self.heads, self.groups)


class Reduction:
    def __init__(self, sizes, rows, used, cuts, done, refs):
        self.sizes, self.rows, self.used = sizes, rows, used
        self.chunk = rows // sizes.groups
        (
            self.out_buf,
            self.head_in,
            self.mid,
            self.dp_in,
            self.total,
            self.head_send,
            self.head_recv,
            self.dp_send,
            self.dp_recv,
            self.all_send,
            self.all_recv,
            self.own_sem,
        ) = refs
        self.done = done
        self.cuts = [0] + list(cuts) + [used]
        self.me = lax.axis_index("head")
        self.group = lax.axis_index("dp")

    @staticmethod
    def scratch(sizes, rows, used, width, parts):
        chunk = rows // sizes.groups
        vm = pltpu.VMEM
        dma = pltpu.SemaphoreType.DMA
        return [
            vm((sizes.heads, used, width), bf16),
            vm((sizes.heads - 1, used, width), bf16),
            vm((rows, width), bf16),
            vm((sizes.groups - 1, chunk, width), bf16),
            vm((chunk, width), bf16),
            dma((parts, sizes.heads - 1)),
            dma((parts, sizes.heads - 1)),
            dma((sizes.groups - 1,)),
            dma((sizes.groups - 1,)),
            dma((sizes.groups - 1,)),
            dma((sizes.groups - 1,)),
            dma((1,)),
        ]

    def head_copy(self, k, i):
        peer = lax.rem(self.me + k, self.sizes.heads)
        span = pl.ds(self.cuts[i], self.cuts[i + 1] - self.cuts[i])
        return pltpu.make_async_remote_copy(
            src_ref=self.out_buf.at[peer, span],
            dst_ref=self.head_in.at[k - 1, span],
            send_sem=self.head_send.at[i, k - 1],
            recv_sem=self.head_recv.at[i, k - 1],
            device_id={"head": peer},
            device_id_type=pl.DeviceIdType.MESH,
        )

    def part(self, index):
        return pl.ds(pl.multiple_of(index * self.chunk, 16), self.chunk)

    def dp_copy(self, k):
        peer = lax.rem(self.group + k, self.sizes.groups)
        return pltpu.make_async_remote_copy(
            src_ref=self.mid.at[self.part(peer)],
            dst_ref=self.dp_in.at[k - 1],
            send_sem=self.dp_send.at[k - 1],
            recv_sem=self.dp_recv.at[k - 1],
            device_id={"dp": peer},
            device_id_type=pl.DeviceIdType.MESH,
        )

    def all_copy(self, k):
        peer = lax.rem(self.group + k, self.sizes.groups)
        return pltpu.make_async_remote_copy(
            src_ref=self.total,
            dst_ref=self.done.at[self.part(self.group)],
            send_sem=self.all_send.at[k - 1],
            recv_sem=self.all_recv.at[k - 1],
            device_id={"dp": peer},
            device_id_type=pl.DeviceIdType.MESH,
        )

    def start_heads(self, i):
        for k in range(1, self.sizes.heads):
            self.head_copy(k, i).start()

    def start_groups(self):
        for i in range(len(self.cuts) - 1):
            for k in range(1, self.sizes.heads):
                self.head_copy(k, i).wait()
        total = self.out_buf[self.me].astype(f32)
        for k in range(1, self.sizes.heads):
            total += self.head_in[k - 1].astype(f32)
        self.mid[: self.used] = total.astype(bf16)
        each_peer(self.sizes.groups, lambda k: self.dp_copy(k).start())

    def start_gather(self):
        each_peer(self.sizes.groups, lambda k: self.dp_copy(k).wait())
        own = self.part(self.group)
        total = self.mid[own].astype(f32)
        for k in range(1, self.sizes.groups):
            total += self.dp_in[k - 1].astype(f32)
        self.total[...] = total.astype(bf16)
        self.own_copy().start()
        each_peer(self.sizes.groups, lambda k: self.all_copy(k).start())

    def own_copy(self):
        return pltpu.make_async_copy(
            self.total, self.done.at[self.part(self.group)], self.own_sem.at[0]
        )

    def finish(self):
        self.own_copy().wait()
        each_peer(self.sizes.groups, lambda k: self.all_copy(k).wait())


def each_peer(count, act):
    def step(k, carry):
        act(k)
        return carry

    if count <= 8:
        for k in range(1, count):
            act(k)
    else:
        lax.fori_loop(1, count, step, 0)


def body(sizes, *refs):
    inputs = 18
    early_refs = refs[inputs : inputs + sizes.layers]
    exchange(sizes, early_refs, *refs[:inputs], *refs[inputs + sizes.layers :])


def exchange(
    sizes,
    early_refs,
    count_ref,
    sample_ref,
    x_ref,
    cot_ref,
    qkv_shard_ref,
    qv_ref,
    out_w_ref,
    up_w_ref,
    down_w_ref,
    g1_ref,
    b1_ref,
    bo_ref,
    g2_ref,
    b2_ref,
    bd_ref,
    bu_ref,
    lo_ref,
    ig_ref,
    late_ref,
    stream,
    xh1,
    rs1,
    n1e,
    qkv,
    v_tok,
    probs,
    inv,
    att,
    xh2,
    rs2,
    n2e,
    act,
    slope,
    qkv_t_ref,
    qkv_n,
    out_t,
    up_t,
    down_t,
    cols,
    mask,
    g_qkv,
    g_out,
    g_up,
    g_down,
    g_vec,
    k_tok,
    g_scr,
    gl_kept,
    gp_kept,
    gm_kept,
    gqkv_kept,
    vec_rows,
    lo_stage,
    ig_stage,
    qv_own,
    qv_all,
    shard_send,
    shard_recv,
    qv_send,
    qv_recv,
    lo_send,
    lo_recv,
    ig_send,
    ig_recv,
    own_sem,
    x_in,
    x_rows,
    cot_t,
    in_sem,
    *reduction_refs,
):
    layers, heads, width, units = sizes.layers, sizes.heads, sizes.width, sizes.units
    win, toks, own, hd, share = sizes.win, sizes.toks, sizes.own, sizes.hd, sizes.share
    scale = 1.0 / math.sqrt(hd)
    half = toks // 2
    abreast = math.gcd(own, group_size)
    me = lax.axis_index("head")
    group = lax.axis_index("dp")
    earlies = [
        Reduction(sizes, rows, used, cuts, early_refs[l], reduction_refs[12 * l : 12 * (l + 1)])
        for l, (used, cuts, rows) in enumerate(sizes.early)
    ]
    late = Reduction(sizes, sizes.late, sizes.late_used, (), late_ref, reduction_refs[12 * layers :])

    def head_peer(k):
        return lax.rem(me + k, heads)

    first = me * own
    fetch_from = pl.multiple_of(first // sizes.block * sizes.block, 16)
    fetches = [
        pltpu.make_async_copy(src.at[:, pl.ds(fetch_from, sizes.block)], dst, in_sem.at[i])
        for i, (src, dst) in enumerate(((x_ref, x_in), (cot_ref, x_in)))
    ]
    fetches[0].start()
    barrier = pltpu.get_barrier_semaphore()
    for k in range(1, heads):
        pl.semaphore_signal(
            barrier, inc=1, device_id={"head": head_peer(k)}, device_id_type=pl.DeviceIdType.MESH
        )

    def greet(k):
        pl.semaphore_signal(
            barrier,
            inc=1,
            device_id={"dp": lax.rem(group + k, sizes.groups)},
            device_id_type=pl.DeviceIdType.MESH,
        )

    each_peer(sizes.groups, greet)

    c_g1, c_b1, c_qkv, c_bo = 0, width, 2 * width, 5 * width
    c_g2, c_b2, c_bd, c_up = 6 * width, 7 * width, 8 * width, 9 * width

    identity = eye(width)
    identity_tok = eye(toks)

    def row_to_column(row):
        return jnp.transpose(jnp.broadcast_to(row, (lane, lane)))

    qv_own[...] = jnp.zeros_like(qv_own)
    for l in range(layers):
        qv_own[l : l + 1, :hd] = qv_ref[l : l + 1, :hd]
        qv_own[l : l + 1, 2 * hd : 3 * hd] = qv_ref[l : l + 1, hd : 2 * hd]
    mine = pl.ds(pl.multiple_of(me * 3 * hd, 16), 3 * hd)
    own_shard = pltpu.make_async_copy(qkv_shard_ref, qkv_t_ref.at[:, mine], own_sem.at[0])
    own_qv = pltpu.make_async_copy(qv_own, qv_all.at[me], own_sem.at[1])

    def shard_copy(k):
        return pltpu.make_async_remote_copy(
            src_ref=qkv_shard_ref,
            dst_ref=qkv_t_ref.at[:, mine],
            send_sem=shard_send.at[k - 1],
            recv_sem=shard_recv.at[k - 1],
            device_id={"head": head_peer(k)},
            device_id_type=pl.DeviceIdType.MESH,
        )

    def qv_copy(k):
        return pltpu.make_async_remote_copy(
            src_ref=qv_own,
            dst_ref=qv_all.at[me],
            send_sem=qv_send.at[k - 1],
            recv_sem=qv_recv.at[k - 1],
            device_id={"head": head_peer(k)},
            device_id_type=pl.DeviceIdType.MESH,
        )

    pl.semaphore_wait(barrier, heads - 1 + sizes.groups - 1)
    own_shard.start()
    own_qv.start()
    for k in range(1, heads):
        qv_copy(k).start()
        shard_copy(k).start()

    def sort_rows(src, dst):
        step = 10 if win % 10 == 0 else 1
        for t in range(0, win, step):
            block = src[t : t + step].astype(f32)
            rows = block[:, :own]
            for i in range(1, sizes.block // own):
                here = first - fetch_from == i * own
                rows = jnp.where(here, block[:, i * own : (i + 1) * own], rows)
            dst[t * own : (t + step) * own] = rows.reshape(step * own, width)
        dst[win * own :] = jnp.zeros(((toks - win) * own, width), f32)

    def turned(src, w):
        return nt(identity, src[pl.ds(w, toks, stride=own), :].astype(bf16))

    def put_column(l, start, ref):
        cols[l, start : start + width] = row_to_column(ref[l : l + 1, :])

    for l in range(layers):
        out_t[l] = nt(identity, out_w_ref[l]).astype(bf16)
        for part in range(units // width):
            span = slice(part * width, (part + 1) * width)
            up_t[l, span, :] = jnp.transpose(up_w_ref[l, :, span].astype(f32)).astype(bf16)
            cols[l, c_up + part * width : c_up + (part + 1) * width] = row_to_column(
                bu_ref[l : l + 1, span]
            )
        down_t[l] = nt(identity, down_w_ref[l]).astype(bf16)
        for start, ref in (
            (c_bo, bo_ref),
            (c_g2, g2_ref),
            (c_b2, b2_ref),
            (c_bd, bd_ref),
        ):
            put_column(l, start, ref)
        put_column(l, c_g1, g1_ref)
        put_column(l, c_b1, b1_ref)
    key_pos = lax.broadcasted_iota(jnp.int32, (half, half), 0)
    query_pos = lax.broadcasted_iota(jnp.int32, (half, half), 1)
    mask[...] = jnp.where(key_pos <= query_pos, 0.0, far_below)
    g_vec[...] = jnp.zeros_like(g_vec)
    vec_rows[...] = jnp.zeros_like(vec_rows)
    for packet in earlies + [late]:
        if packet.rows > packet.used:
            packet.mid[packet.used :] = jnp.zeros((packet.rows - packet.used, width), bf16)

    for w in range(own):
        for l in range(layers):
            n1e[l, w, width:, :] = jnp.ones((ones_rows, toks), bf16)
            n2e[l, w, width:, :] = jnp.ones((ones_rows, toks), bf16)
            att[l, w, width:, :] = jnp.ones((ones_rows, toks), bf16)
            act[l, w, units:, :] = jnp.ones((ones_rows, toks), bf16)
        for h in range(heads):
            g_scr[w, h, half:, :half] = jnp.zeros((half, half), bf16)
            for l in range(layers):
                probs[l, w, h, half:, :half] = jnp.zeros((half, half), bf16)

    fetches[0].wait()
    sort_rows(x_in, x_rows)
    fetches[1].start()
    for w in range(own):
        stream[w] = turned(x_rows, w)

    fetches[1].wait()
    sort_rows(x_in, x_rows)
    for w in range(own):
        cot_t[w] = turned(x_rows, w).astype(bf16)

    def col(l, start, count):
        return wide(cols[l, start : start + count, :], toks)

    step = hd


    def spans(start, count):
        return [slice(r, r + step) for r in range(start, start + count, step)]

    def norm(w, l, gain, shift, unit_ref, spread_ref, low_ref):
        total = sum(fold(stream[w, r], jnp.add) for r in spans(0, width))
        mean = jnp.sum(total, axis=0, keepdims=True) * (1.0 / width)
        square = 0.0
        for r in spans(0, width):
            center = stream[w, r] - mean
            square += fold(center * center, jnp.add)
        spread = lax.rsqrt(jnp.sum(square, axis=0, keepdims=True) * (1.0 / width) + norm_eps)
        spread_ref[l, w] = spread
        for r in spans(0, width):
            unit = (stream[w, r] - mean) * spread
            unit_ref[l, w, r] = unit
            low_ref[l, w, r] = (
                unit * col(l, gain + r.start, step) + col(l, shift + r.start, step)
            ).astype(bf16)

    for w in range(own):
        norm(w, 0, c_g1, c_b1, xh1, rs1, n1e)
    own_shard.wait()
    own_qv.wait()
    for k in range(1, heads):
        qv_copy(k).wait()
        shard_copy(k).wait()
    for l in range(layers):
        qkv_n[l] = nt(identity, qkv_t_ref[l]).astype(bf16)
        for h in range(heads):
            cols[l, c_qkv + 3 * hd * h : c_qkv + 3 * hd * (h + 1)] = row_to_column(
                qv_all[h, l : l + 1, :]
            )[: 3 * hd]
    def forward(l, w):
        if l:
            norm(w, l, c_g1, c_b1, xh1, rs1, n1e)
            yield
        made = nn(qkv_t_ref[l], n1e[l, w, :width])
        for i, r in enumerate(spans(0, 3 * width)):
            piece = made[r] + col(l, c_qkv + r.start, step)
            qkv[l, w, r] = (piece if i % 3 else piece * (scale * log2_e)).astype(bf16)
        yield
        rows_of = lambda h, which: slice((3 * h + which) * hd, (3 * h + which + 1) * hd)
        kv_all = jnp.concatenate(
            [qkv[l, w, rows_of(h, which)] for which in (1, 2) for h in range(heads)], axis=0
        )
        turned_kv = jnp.transpose(kv_all)
        k_tok[w] = turned_kv[:, :width]
        v_tok[l, w] = turned_kv[:, width:]
        for h in range(heads):
            yield
            s = nn(k_tok[w], spread_rows(qkv[l, w, rows_of(h, 0)], h, heads))
            top0 = top1 = None
            for r in spans(0, half):
                far = slice(r.start + half, r.stop + half)
                new0 = fold(s[r, :half] + mask[r], jnp.maximum)
                new1 = jnp.maximum(
                    fold(s[r, half:], jnp.maximum), fold(s[far, half:] + mask[r], jnp.maximum)
                )
                top0 = new0 if top0 is None else jnp.maximum(top0, new0)
                top1 = new1 if top1 is None else jnp.maximum(top1, new1)
            top0 = jnp.max(top0, axis=0, keepdims=True)
            top1 = jnp.max(top1, axis=0, keepdims=True)
            for r in spans(0, half):
                far = slice(r.start + half, r.stop + half)
                probs[l, w, h, r, :half] = jnp.exp2(s[r, :half] + mask[r] - top0).astype(bf16)
                probs[l, w, h, r, half:] = jnp.exp2(s[r, half:] - top1).astype(bf16)
                probs[l, w, h, far, half:] = jnp.exp2(s[far, half:] + mask[r] - top1).astype(bf16)
            yield
            v_ext = jnp.concatenate(
                [qkv[l, w, rows_of(h, 2)], jnp.ones((ones_rows, toks), bf16)], axis=0
            )
            o = nn(v_ext, probs[l, w, h])
            inverse = 1.0 / o[hd : hd + 1]
            inv[l, w, h] = inverse
            att[l, w, hd * h : hd * (h + 1)] = (o[:hd] * inverse).astype(bf16)
        yield
        made = nn(out_t[l], att[l, w, :width])
        for r in spans(0, width):
            stream[w, r] = stream[w, r] + made[r] + col(l, c_bo + r.start, step)
        norm(w, l, c_g2, c_b2, xh2, rs2, n2e)
        yield
        made = nn(up_t[l], n2e[l, w, :width])
        for r in spans(0, units):
            a, sl = gelu_parts(made[r] + col(l, c_up + r.start, step))
            act[l, w, r] = a.astype(bf16)
            slope[l, w, r] = sl.astype(bf16)
        yield
        made = nn(down_t[l], act[l, w, :units])
        for r in spans(0, width):
            value = stream[w, r] + made[r] + col(l, c_bd + r.start, step)
            if l < layers - 1:
                stream[w, r] = value
            else:
                lo_stage[r.start // hd, w] = value.astype(bf16)

    def norm_sums(l, w, grad, gain, unit_ref, which):
        plain = tilted = 0.0
        for r in spans(0, width):
            by_unit = grad[r] * unit_ref[l, w, r]
            at = slice(which * width + r.start, which * width + r.stop)
            g_vec[l, at] += by_unit
            at = slice((which + 1) * width + r.start, (which + 1) * width + r.stop)
            g_vec[l, at] += grad[r]
            column = col(l, gain + r.start, step)
            plain += fold(grad[r] * column, jnp.add)
            tilted += fold(by_unit * column, jnp.add)
        return (
            jnp.sum(plain, axis=0, keepdims=True) * (1.0 / width),
            jnp.sum(tilted, axis=0, keepdims=True) * (1.0 / width),
        )

    def norm_back(l, w, grad, gain, unit_ref, spread_ref, means, emit):
        spread = spread_ref[l, w]
        for r in spans(0, width):
            s = grad[r] * col(l, gain + r.start, step)
            emit(r, stream[w, r] + spread * (s - means[0] - unit_ref[l, w, r] * means[1]))

    def backward_units(l, w):
        if l == layers - 1:
            slot = me * own + w
            weight = jnp.where(slot < count_ref[0], sample_ref[slot], 0.0)
        for r in spans(0, width):
            if l == layers - 1:
                stream[w, r] = cot_t[w, r].astype(f32) * weight
            gl_kept[w, r] = stream[w, r].astype(bf16)
        yield
        made = nn(down_w_ref[l], gl_kept[w])
        for r in spans(0, units):
            gp_kept[w, r] = made[r].astype(bf16) * slope[l, w, r]
        yield
        gn = nn(up_w_ref[l], gp_kept[w])
        yield
        means = norm_sums(l, w, gn, c_g2, xh2, 2)

        def emit(r, value):
            stream[w, r] = value
            gm_kept[w, r] = value.astype(bf16)

        norm_back(l, w, gn, c_g2, xh2, rs2, means, emit)

    def backward_attention(l, w, after):
        ga = nn(out_w_ref[l], gm_kept[w])
        shares, dots = [], []
        for h in range(heads):
            rows = slice(h * hd, (h + 1) * hd)
            gs = (ga[rows] * inv[l, w, h]).astype(bf16)
            shares.append(gs)
            dots.append(
                jnp.sum(gs.astype(f32) * att[l, w, rows, :].astype(f32), axis=0, keepdims=True)
            )
        yield
        for h in range(heads):
            base = 3 * h * hd
            yield
            gs, dot = shares[h], dots[h]
            made = nn(v_tok[l, w], spread_rows(gs, h, heads))
            gqkv_kept[w, base + 2 * hd : base + 3 * hd] = nt(gs, probs[l, w, h]).astype(bf16)
            d0, d1 = dot[:, :half], dot[:, half:]
            for r in spans(0, half):
                far = slice(r.start + half, r.stop + half)
                g_scr[w, h, r, :half] = probs[l, w, h, r, :half] * (made[r, :half] - d0).astype(bf16)
                g_scr[w, h, r, half:] = probs[l, w, h, r, half:] * (made[r, half:] - d1).astype(bf16)
                g_scr[w, h, far, half:] = probs[l, w, h, far, half:] * (
                    made[far, half:] - d1
                ).astype(bf16)
            yield
            q = qkv[l, w, base : base + hd, :]
            k = qkv[l, w, base + hd : base + 2 * hd, :]
            g = g_scr[w, h]
            gq = (nn(k, g) * scale).astype(bf16)
            gk = (nt(q, g) * (1.0 / log2_e)).astype(bf16)
            gqkv_kept[w, base : base + hd] = gq
            gqkv_kept[w, base + hd : base + 2 * hd] = gk
        yield
        gn = nn(qkv_n[l], gqkv_kept[w])
        yield
        means = norm_sums(l, w, gn, c_g1, xh1, 0)
        after(w, gn, means)

    def lanes(ref, ws):
        return jnp.concatenate([ref[w] for w in ws], axis=1)

    def unit_sums(l, ws):
        def add(ref, value):
            ref[l] = value if ws[0] == 0 else ref[l] + value

        add(g_down, nt(lanes(act.at[l], ws), lanes(gl_kept, ws)))
        add(g_up, nt(lanes(n2e.at[l], ws), lanes(gp_kept, ws)))
        add(g_out, nt(lanes(att.at[l], ws), lanes(gm_kept, ws)))

    def qkv_sums(l, ws):
        value = nt(lanes(gqkv_kept, ws), lanes(n1e.at[l], ws))
        g_qkv[l] = value if ws[0] == 0 else g_qkv[l] + value

    def run(step, first, last, width=1):
        def inner(i, carry):
            side_by_side([step(first + i * width + u) for u in range(width)])
            return carry

        if last - first == width:
            inner(0, 0)
        else:
            lax.fori_loop(0, (last - first) // width, inner, 0)

    last = math.gcd(own, 4)
    cut = own - last

    def lo_copy(k):
        peer = head_peer(k)
        return pltpu.make_async_remote_copy(
            src_ref=lo_stage.at[peer],
            dst_ref=lo_ref.at[pl.ds(me * own, own)],
            send_sem=lo_send.at[k - 1],
            recv_sem=lo_recv.at[k - 1],
            device_id={"head": peer},
            device_id_type=pl.DeviceIdType.MESH,
        )

    def ig_copy(k, i):
        peer = head_peer(k)
        return pltpu.make_async_remote_copy(
            src_ref=ig_stage.at[peer, pl.ds(i * last, last)],
            dst_ref=ig_ref.at[pl.ds(me * own + i * last, last)],
            send_sem=ig_send.at[k - 1, i],
            recv_sem=ig_recv.at[k - 1, i],
            device_id={"head": peer},
            device_id_type=pl.DeviceIdType.MESH,
        )

    for l in range(layers):
        run(functools.partial(forward, l), 0, own, abreast)

    own_lo = pltpu.make_async_copy(
        lo_stage.at[me], lo_ref.at[pl.ds(me * own, own)], own_sem.at[2]
    )
    own_lo.start()
    for k in range(1, heads):
        lo_copy(k).start()

    def vector_rows(l, norm_index):
        at = slice(2 * norm_index * width, 2 * (norm_index + 1) * width)
        return nt_split(jnp.ones((16, toks), bf16), g_vec[l, at])

    def qkv_bias_rows(l):
        at = lax.broadcasted_iota(jnp.int32, (16, width + ones_rows), 1)
        return nt_split((at == width).astype(f32).astype(bf16), g_qkv[l])

    def pack_units(l):
        buf = earlies[l].out_buf
        for h in range(heads):
            at = 0
            buf[h, at : at + hd] = g_out[l, hd * h : hd * (h + 1), :].astype(bf16)
            at += hd
            buf[h, at : at + width] = g_up[l, :width, share * h : share * (h + 1)].astype(bf16)
            at += width
            buf[h, at : at + share] = g_down[l, share * h : share * (h + 1), :].astype(bf16)

    def pack_qkv(l):
        r = sizes.first_rows
        for h in range(heads):
            earlies[l].out_buf[h, r : r + 3 * hd] = g_qkv[
                l, 3 * hd * h : 3 * hd * (h + 1), :width
            ].astype(bf16)

    def put_row(at, row):
        for h in range(heads):
            vec_rows[h, at : at + 1] = row

    def put_norm(l, norm_index, at):
        sums = vector_rows(l, norm_index)
        put_row(at, sums[:1, :width])
        put_row(at + 1, sums[:1, width:])

    def put_qkv(l):
        biases = qkv_bias_rows(l)
        for h in range(heads):
            for i in range(3):
                at = (3 * h + i) * hd
                vec_rows[h, 8 * l + 7 : 8 * l + 8, i * hd : (i + 1) * hd] = biases[:1, at : at + hd]

    def pack_vectors():
        for l in range(layers):
            v = 8 * l
            if l:
                put_norm(l, 0, v)
                put_qkv(l)
            put_row(v + 2, g_out[l, width : width + 1, :])
            put_norm(l, 1, v + 3)
            put_row(v + 5, g_down[l, units : units + 1, :])
            for h in range(heads):
                vec_rows[h, v + 6 : v + 7] = g_up[
                    l, width : width + 1, share * h : share * (h + 1)
                ]

    def pack_late():
        put_norm(0, 0, 0)
        put_qkv(0)
        for h in range(heads):
            late.out_buf[h, : 3 * hd] = g_qkv[0, 3 * hd * h : 3 * hd * (h + 1), :width].astype(
                bf16
            )
            late.out_buf[h, 3 * hd :] = vec_rows[h].astype(bf16)

    def give(w, gn, means):
        def emit(r, value):
            ig_stage[r.start // hd, w] = value.astype(bf16)

        norm_back(0, w, gn, c_g1, xh1, rs1, means, emit)
    waiting = {}

    def keep(w, gn, means):
        for i in range(toks // lane):
            at = (w * (toks // lane) + i) * width
            x_rows[at : at + width] = gn[:, i * lane : (i + 1) * lane]
        waiting[w] = means

    everyone = list(range(own))
    for l in range(layers - 1, -1, -1):
        run(functools.partial(backward_units, l), 0, own, abreast)
        steps = {}
        if l < layers - 1:
            steps[heads + 2] = earlies[l + 1].start_gather
        if l:

            def settle(w, gn, means, l=l):
                def emit(r, value):
                    stream[w, r] = value

                norm_back(l, w, gn, c_g1, xh1, rs1, means, emit)

            def unit_step(l=l):
                unit_sums(l, everyone)
                pack_units(l)
                earlies[l].start_heads(0)

            steps[heads] = unit_step
        else:
            settle = keep
            unit_sums(l, everyone)
            pack_units(l)
            earlies[l].start_heads(0)
            steps[2] = pack_vectors
            steps[2 * heads] = earlies[l].start_groups
        if l < layers - 1:
            earlies[l + 1].start_groups()
        side_by_side([backward_attention(l, w, after=settle) for w in everyone], steps)
        if l:
            qkv_sums(l, everyone)
            pack_qkv(l)
            earlies[l].start_heads(1)

    qkv_sums(0, everyone)
    pack_late()
    late.start_heads(0)
    earlies[0].start_gather()
    batches = own // last

    def give_batch(i):
        for w in everyone[i * last : (i + 1) * last]:
            at = w * (toks // lane) * width
            halves = [x_rows[at + i * width : at + (i + 1) * width] for i in range(toks // lane)]
            give(w, jnp.concatenate(halves, axis=1), waiting[w])

    def send_batch(i):
        for k in range(1, heads):
            ig_copy(k, i).start()

    for i in range(batches - 1):
        give_batch(i)
        send_batch(i)
    give_batch(batches - 1)
    own_ig = pltpu.make_async_copy(
        ig_stage.at[me], ig_ref.at[pl.ds(me * own, own)], own_sem.at[3]
    )
    late.start_groups()
    send_batch(batches - 1)
    own_ig.start()
    own_lo.wait()
    for k in range(1, heads):
        lo_copy(k).wait()
    late.start_gather()
    for packet in earlies:
        packet.finish()
    for i in range(batches):
        for k in range(1, heads):
            ig_copy(k, i).wait()
    own_ig.wait()
    late.finish()


def finish_body(sizes, lo_in, ig_in, *refs):
    packets = refs[: sizes.layers + 1]
    write_outputs(sizes, lo_in, ig_in, packets[:-1], packets[-1], *refs[sizes.layers + 1 :])


def write_outputs(
    sizes,
    lo_in,
    ig_in,
    earlies_in,
    late_in,
    lo_out,
    ig_out,
    ln1_g,
    ln1_s,
    qkv_g,
    qv_g,
    out_g,
    out_b,
    ln2_g,
    ln2_s,
    up_g,
    up_b,
    down_g,
    down_b,
):
    hd, width, share = sizes.hd, sizes.width, sizes.share
    lo_out[...] = lo_in[...][:, :, : sizes.win]
    ig_out[...] = ig_in[...][:, :, : sizes.win].astype(f32)
    for l in range(sizes.layers):
        at = 0
        early_in = earlies_in[l]
        out_g[l] = early_in[at : at + hd].astype(f32)
        at += hd
        up_g[l] = early_in[at : at + width].astype(f32)
        at += width
        down_g[l] = early_in[at : at + share].astype(f32)
        at += share
        if l:
            qkv_g[l] = early_in[at : at + 3 * hd].astype(f32)
            at += 3 * hd
        else:
            qkv_g[l] = late_in[: 3 * hd].astype(f32)
    vec = late_in[3 * hd : 3 * hd + sizes.vec].astype(f32)
    for l in range(sizes.layers):
        v = 8 * l
        row = slice(l, l + 1)
        ln1_g[row] = vec[v : v + 1]
        ln1_s[row] = vec[v + 1 : v + 2]
        out_b[row] = vec[v + 2 : v + 3]
        ln2_g[row] = vec[v + 3 : v + 4]
        ln2_s[row] = vec[v + 4 : v + 5]
        down_b[row] = vec[v + 5 : v + 6]
        up_b[row] = vec[v + 6 : v + 7]
        qv = vec[v + 7 : v + 8]
        qv_g[row, :hd] = qv[:, :hd]
        qv_g[row, hd:] = qv[:, 2 * hd : 3 * hd]


def exchange_pass(sizes, count, sample, x, cot, shard, qv, big, small):
    layers, heads, width, units = sizes.layers, sizes.heads, sizes.width, sizes.units
    own, toks, hd, win = sizes.own, sizes.toks, sizes.hd, sizes.win
    vm = lambda *shape: pltpu.VMEM(shape[:-1], shape[-1])
    dma = pltpu.SemaphoreType.DMA
    whole = pl.BlockSpec(memory_space=pltpu.VMEM)
    scalars = pl.BlockSpec(memory_space=pltpu.SMEM)
    left = pl.BlockSpec(memory_space=pl.ANY)
    return pl.pallas_call(
        functools.partial(body, sizes),
        out_shape=(
            jax.ShapeDtypeStruct((sizes.slots, hd, toks), bf16),
            jax.ShapeDtypeStruct((sizes.slots, hd, toks), bf16),
            *[jax.ShapeDtypeStruct((rows, width), bf16) for _, _, rows in sizes.early],
            jax.ShapeDtypeStruct((sizes.late, width), bf16),
        ),
        in_specs=[scalars, scalars, left, left] + [whole] * 12,
        out_specs=(left,) * (layers + 3),
        scratch_shapes=[
            vm(own, width, toks, f32),
            vm(layers, own, width, toks, f32),
            vm(layers, own, 1, toks, f32),
            vm(layers, own, width + ones_rows, toks, bf16),
            vm(layers, own, 3 * width, toks, bf16),
            vm(layers, own, toks, width, bf16),
            vm(layers, own, heads, toks, toks, bf16),
            vm(layers, own, heads, 1, toks, f32),
            vm(layers, own, width + ones_rows, toks, bf16),
            vm(layers, own, width, toks, f32),
            vm(layers, own, 1, toks, f32),
            vm(layers, own, width + ones_rows, toks, bf16),
            vm(layers, own, units + ones_rows, toks, bf16),
            vm(layers, own, units, toks, bf16),
            vm(layers, 3 * width, width, bf16),
            vm(layers, width, 3 * width, bf16),
            vm(layers, width, width, bf16),
            vm(layers, units, width, bf16),
            vm(layers, width, units, bf16),
            vm(layers, 9 * width + units, lane, f32),
            vm(toks // 2, toks // 2, f32),
            vm(layers, 3 * width, width + ones_rows, f32),
            vm(layers, width + ones_rows, width, f32),
            vm(layers, width + ones_rows, units, f32),
            vm(layers, units + ones_rows, width, f32),
            vm(layers, 4 * width, toks, f32),
            vm(own, toks, width, bf16),
            vm(own, heads, toks, toks, bf16),
            vm(own, width, toks, bf16),
            vm(own, units, toks, bf16),
            vm(own, width, toks, bf16),
            vm(own, 3 * width, toks, bf16),
            vm(heads, sizes.vec, width, f32),
            vm(heads, own, hd, toks, bf16),
            vm(heads, own, hd, toks, bf16),
            vm(8, lane, f32),
            vm(heads, 8, lane, f32),
            dma((heads - 1,)),
            dma((heads - 1,)),
            dma((heads - 1,)),
            dma((heads - 1,)),
            dma((heads - 1,)),
            dma((heads - 1,)),
            dma((heads - 1, own)),
            dma((heads - 1, own)),
            dma((4,)),
            vm(win, sizes.block, width, bf16),
            vm(toks * own, width, f32),
            vm(own, width, toks, bf16),
            dma((2,)),
        ]
        + [
            ref
            for used, cuts, rows in sizes.early
            for ref in Reduction.scratch(sizes, rows, used, width, len(cuts) + 1)
        ]
        + Reduction.scratch(sizes, sizes.late, sizes.late_used, width, 1),
        compiler_params=pltpu.CompilerParams(
            vmem_limit_bytes=63 * 1024 * 1024, collective_id=0, has_side_effects=True
        ),
    )(count, sample, x, cot, shard, qv, *big, *small)


def finish_pass(sizes, lo, ig, *packets):
    layers, width, hd, share = sizes.layers, sizes.width, sizes.hd, sizes.share
    whole = pl.BlockSpec(memory_space=pltpu.VMEM)
    out = lambda *shape: jax.ShapeDtypeStruct(shape, f32)
    row = out(layers, width)
    final = (sizes.slots, hd, sizes.win)
    return pl.pallas_call(
        functools.partial(finish_body, sizes),
        out_shape=(
            jax.ShapeDtypeStruct(final, bf16),
            out(*final),
            row,
            row,
            out(layers, 3 * hd, width),
            out(layers, 2 * hd),
            out(layers, hd, width),
            row,
            row,
            row,
            out(layers, width, share),
            out(layers, share),
            out(layers, share, width),
            row,
        ),
        in_specs=[whole] * (2 + len(packets)),
        out_specs=(whole,) * 14,
        compiler_params=pltpu.CompilerParams(vmem_limit_bytes=60 * 1024 * 1024),
    )(lo, ig, *packets)


def shards(
    layer_input,
    cotangent,
    window_count,
    sample_weight,
    ln1_gain,
    ln1_shift,
    qkv_weight,
    qv_bias,
    out_weight,
    out_bias,
    ln2_gain,
    ln2_shift,
    up_weight,
    up_bias,
    down_weight,
    down_bias,
):
    slots, win, width = layer_input.shape
    layers, _, units = up_weight.shape
    sizes = Sizes(
        slots, win, width, layers, units, lax.axis_size("head"), lax.axis_size("dp")
    )
    lo, ig, *packets = exchange_pass(
        sizes,
        window_count,
        sample_weight,
        jnp.swapaxes(layer_input, 0, 1),
        jnp.swapaxes(cotangent, 0, 1),
        jnp.swapaxes(qkv_weight, 1, 2),
        qv_bias,
        (out_weight, up_weight, down_weight),
        (ln1_gain, ln1_shift, out_bias, ln2_gain, ln2_shift, down_bias, up_bias),
    )
    outs = list(finish_pass(sizes, lo, ig, *packets))
    for index in (0, 1, 4):
        outs[index] = jnp.swapaxes(outs[index], 1, 2)
    return tuple(outs)


def solution(mesh):
    return jax.shard_map(
        shards,
        mesh=mesh,
        in_specs=(
            P("dp", None, None),
            P("dp", None, None),
            P("dp"),
            P("dp"),
            P(),
            P(),
            P(None, None, "head"),
            P(None, "head"),
            P(),
            P(),
            P(),
            P(),
            P(),
            P(),
            P(),
            P(),
        ),
        out_specs=(
            P("dp", None, "head"),
            P("dp", None, "head"),
            P(),
            P(),
            P(None, None, "head"),
            P(None, "head"),
            P(None, "head", None),
            P(),
            P(),
            P(),
            P(None, None, "head"),
            P(None, "head"),
            P(None, "head", None),
            P(),
        ),
        check_vma=False,
    )
```
